32 devices in a mesh: blk: 8 (over z, x), col: 4 (over y, core).
Axes of the slice: x: 2, y: 2, z: 4, core: 2. Of those that a mesh axis runs over, the one named last changes fastest.
Arguments:
- slab: float32 [16384, 1024], P('blk', 'col'), may hold values from -6 to 6
- angles: float32 [4, 8192], P(None, 'blk'), may hold values from -3.140625 to 3.140625
- pairing: int32 [4], replicated, may hold values from 0 to 1, as said below
- band_offsets: int32 [8], replicated, may hold values from 1 to 512, as said below
- band_weights: float32 [8], replicated, may hold values from -0.0625 to 0.0625
Outputs:
- evolved: float32 [16384, 1024], P('blk', 'col')
- angle_gradient: float32 [4, 8192], P(None, 'blk')
The draws below stay inside these ranges and needn't reach their ends.
Inputs may be any that keep to these rules, and one draw needn't show every extreme that they name: `pairing`: the entries alternate between 0 and 1 from one layer to the next. `band_offsets`: exactly one entry equals 512.
All inputs are finite; a program needn't handle non-finite values.
Results may differ from the reference program's by a relative error of at most 0.0001.
Values sent between devices are 32-bit elements; how exact they have to be, the bound alone decides.
A program may use at most 128 MiB of HBM per device.

```python
import jax
import jax.numpy as jnp

LAYERS = 4
REACH = 512
BANDS = 8
ROWS = 16384
PAIRS = 8192
SLAB_COLS = 1024


def draw_pairing(key, part):
    leading = jax.random.randint(jax.random.fold_in(key, 7), (), 0, 2)
    steps = jnp.arange(LAYERS, dtype=jnp.int32)
    return ((steps + leading) % 2).astype(jnp.int32)


def draw_band_offsets(key, part):
    values = jax.random.randint(jax.random.fold_in(key, 11), (BANDS,), 1, REACH)
    where = jax.random.randint(jax.random.fold_in(key, 13), (), 0, BANDS)
    slots = jnp.arange(BANDS, dtype=jnp.int32)
    return jnp.where(slots == where, REACH, values).astype(jnp.int32)


def steps_of(stream_key, extent, shards, least, high):
    def one(dim, blocks):
        steps = jax.random.uniform(jax.random.fold_in(jax.random.fold_in(stream_key, 6), dim), (blocks,), jnp.float32, least / len(shards), high / len(shards))
        return jnp.repeat(jnp.exp(steps), extent[dim] // blocks).reshape((-1,) + (1,) * (len(extent) - dim - 1))

    factor_of = one(*shards[0])
    for cut in shards[1:]:
        factor_of = factor_of * one(*cut)
    return factor_of


def normal_values(key, extent, deviation, most, pieces=(), kind=jnp.bfloat16):
    level = steps_of(key, extent, pieces, -0.22, 0.18) if pieces else 1.0
    values = jax.random.normal(key, extent, jnp.float32) * deviation * level
    return jnp.minimum(jnp.maximum(values, -most), most).astype(kind)


def setup_inputs(seed: int = 0) -> dict:
    splits = jax.random.split(jax.random.key(seed), 6)
    slab = normal_values(splits[0], (ROWS, SLAB_COLS), 1.0, 6.0, ((0, 8), (1, 4)), jnp.float32)
    angles = jnp.clip(jax.random.uniform(splits[1], (LAYERS, PAIRS), jnp.float32, -3.140625, 3.140625), -3.140625, 3.140625)
    pairing = draw_pairing(jax.random.fold_in(splits[5], 71), 0)
    band_offsets = draw_band_offsets(jax.random.fold_in(splits[5], 71), 0)
    band_weights = normal_values(splits[4], (BANDS,), (BANDS * SLAB_COLS) ** -0.5, 0.0625, (), jnp.float32)
    return dict(slab=slab, angles=angles, pairing=pairing, band_offsets=band_offsets, band_weights=band_weights)


def rotate(field, offset, cosine, sine):
    rolled = jnp.roll(field, -offset, 0).reshape(field.shape[0] // 2, 2, field.shape[1])
    first = rolled[:, 0]
    second = rolled[:, 1]
    new_first = cosine[:, None] * first - sine[:, None] * second
    new_second = sine[:, None] * first + cosine[:, None] * second
    flat = jnp.stack([new_first, new_second], 1).reshape(field.shape)
    return jnp.roll(flat, offset, 0)


def reference(slab, angles, pairing, band_offsets, band_weights):
    state = slab
    after = []
    for layer in range(LAYERS):
        state = rotate(state, pairing[layer], jnp.cos(angles[layer]), jnp.sin(angles[layer]))
        after.append(state)
    adjoint = jnp.zeros_like(state)
    for band in range(BANDS):
        shift = band_offsets[band]
        adjoint = adjoint + band_weights[band] * (jnp.roll(state, -shift, 0) + jnp.roll(state, shift, 0))
    grads = [None] * LAYERS
    for layer in reversed(range(LAYERS)):
        offset = pairing[layer]
        rolled_state = jnp.roll(after[layer], -offset, 0).reshape(ROWS // 2, 2, SLAB_COLS)
        rolled_adj = jnp.roll(adjoint, -offset, 0).reshape(ROWS // 2, 2, SLAB_COLS)
        grads[layer] = jnp.sum(rolled_adj[:, 1] * rolled_state[:, 0] - rolled_adj[:, 0] * rolled_state[:, 1], axis=1)
        adjoint = rotate(adjoint, offset, jnp.cos(angles[layer]), -jnp.sin(angles[layer]))
    return state, jnp.stack(grads)
```

```python
import functools

import jax
import jax.numpy as jnp
from jax import lax
from jax.experimental import pallas as pl
from jax.experimental.pallas import tpu as pltpu
from jax.sharding import PartitionSpec as P

LAYERS = 4
BANDS = 8
REACH = 512
HALF = REACH // 2
SENT = HALF + 8
LANES = 128
FRONT = SENT + 8
STEP = 48
MESH = pl.DeviceIdType.MESH


def sweep(low, high, step, body):
    assert (high - low) % step == 0 and low % 8 == 0 and step % 8 == 0

    def one(i, carry):
        body(pl.multiple_of(low + i * step, 8))
        return carry

    lax.fori_loop(0, (high - low) // step, one, 0)


def kernel(
    nblk, ncol,
    pairing, offsets, weights, slab, angles,
    out, grad,
    raw, land, angw, coef, sa, sb, field, adj, xa, xb, prod, stage, window,
    own_g, left_g, right_g, send_l, send_r,
    load_sem, ang_sem, out_sem, h_send, h_recv, a_send, a_recv, o_send, o_recv, l_send, l_recv, r_send, r_recv,
):
    rows, width = slab.shape
    halves = width // LANES
    pairs = rows // 2
    q_own = HALF
    q_end = q_own + pairs
    q_lo, q_hi = 120, q_end + 136
    total_q = pairs + REACH
    blk = lax.axis_index("blk")
    col = lax.axis_index("col")
    after = lax.rem(blk + 1, nblk)
    before = lax.rem(blk + nblk - 1, nblk)
    others = [lax.rem(col + d, ncol) for d in range(1, ncol)]
    every = [col] + others

    barrier = pltpu.get_barrier_semaphore()
    peers = [(blk, c) for c in others] + [(b, c) for b in (after, before) for c in every]
    for peer in peers:
        pl.semaphore_signal(barrier, inc=1, device_id=peer, device_id_type=MESH)

    loads = []
    for h in range(halves):
        loads.append(pltpu.make_async_copy(
            slab.at[:, pl.ds(h * LANES, LANES)], raw.at[h, pl.ds(FRONT, rows)], load_sem.at[h]))
    own_ang = pltpu.make_async_copy(angles, angw.at[:, pl.ds(HALF, pairs)], ang_sem)
    own_ang.start()
    for load in loads:
        load.start()

    def remote(src, dst, s, r, peer):
        return pltpu.make_async_remote_copy(
            src_ref=src, dst_ref=dst, send_sem=s, recv_sem=r, device_id=peer, device_id_type=MESH)

    ang_copies = [
        remote(angles.at[:, pl.ds(pairs - HALF, HALF)], angw.at[:, pl.ds(0, HALF)], a_send.at[0], a_recv.at[0], (after, col)),
        remote(angles.at[:, pl.ds(0, HALF)], angw.at[:, pl.ds(q_end, HALF)], a_send.at[1], a_recv.at[1], (before, col)),
    ]
    halo_copies = []
    for h in range(halves):
        lanes = pl.ds(h * LANES, LANES)
        halo_copies.append([
            remote(slab.at[pl.ds(rows - SENT, SENT), lanes], land.at[h, 0], h_send.at[h, 0], h_recv.at[h, 0], (after, col)),
            remote(slab.at[pl.ds(0, SENT), lanes], land.at[h, 1], h_send.at[h, 1], h_recv.at[h, 1], (before, col)),
        ])

    pl.semaphore_wait(barrier, len(peers))
    for copy in ang_copies:
        copy.start()
    for pair in halo_copies:
        for copy in pair:
            copy.start()

    first = pairing[0]

    def zeros(n):
        return jnp.zeros((n, LANES), jnp.float32)

    for h in range(halves):
        raw[h, 0:8, :] = zeros(8)
        raw[h, FRONT + rows + SENT:FRONT + rows + SENT + 16, :] = zeros(16)
        adj[h, 2 * q_lo:REACH - HALF, :] = zeros(REACH - HALF - 2 * q_lo)
        top = REACH + rows + HALF
        adj[h, top:2 * q_hi + 8, :] = zeros(2 * q_hi + 8 - top)
        field[h, 0:2 * q_lo + 8, :] = zeros(2 * q_lo + 8)
        field[h, 2 * q_hi:, :] = zeros(field.shape[1] - 2 * q_hi)
        for l in range(LAYERS):
            sa[h, l, q_hi:q_hi + 8, :] = zeros(8)
            sb[h, l, q_lo - 8:q_lo, :] = zeros(8)
            prod[h, l, 0:q_lo, :] = zeros(q_lo)
            prod[h, l, q_hi:total_q, :] = zeros(total_q - q_hi)
        for l in range(LAYERS - 1):
            xb[h, l, q_lo - 8:q_lo, :] = zeros(8)
            xa[h, l, q_hi:q_hi + 8, :] = zeros(8)

    own_ang.wait()
    for copy in ang_copies:
        copy.wait()
    theta = angw[...]
    both = jnp.concatenate([jnp.cos(theta), jnp.sin(theta)], 0)
    rolled = pltpu.roll(both, total_q - 1, 1)
    odd = lax.broadcasted_iota(jnp.int32, both.shape, 0) % 2 == 1
    moved = jnp.full(both.shape, first, jnp.int32) == 1
    window[...] = jnp.where(jnp.logical_and(odd, moved), rolled, both)

    def spread(q):
        part = window[:, pl.ds(pl.multiple_of(q, LANES), LANES)]
        turned = part.T
        for j in range(2 * LAYERS):
            coef[j, pl.ds(q, LANES), :] = jnp.broadcast_to(turned[:, j:j + 1], (LANES, LANES))

    sweep(0, total_q, LANES, spread)

    def forward(h, low, high, step):
        for l in range(LAYERS):
            def body(q, l=l):
                if l == 0:
                    a = raw[h, pl.ds(2 * q - 2 * q_lo + first, step, stride=2), :]
                    b = raw[h, pl.ds(2 * q - 2 * q_lo + 1 + first, step, stride=2), :]
                elif l % 2 == 1:
                    a = sb[h, l - 1, pl.ds(q, step), :]
                    b = sa[h, l - 1, pl.ds(q + 1, step), :]
                else:
                    a = sb[h, l - 1, pl.ds(q - 1, step), :]
                    b = sa[h, l - 1, pl.ds(q, step), :]
                c = coef[l, pl.ds(q, step), :]
                s = coef[LAYERS + l, pl.ds(q, step), :]
                new_a = c * a - s * b
                new_b = s * a + c * b
                sa[h, l, pl.ds(q, step), :] = new_a
                sb[h, l, pl.ds(q, step), :] = new_b
                if l == LAYERS - 1:
                    field[h, pl.ds(2 * q + 1, step, stride=2), :] = new_a
                    field[h, pl.ds(2 * q + 2, step, stride=2), :] = new_b
            sweep(low, high, step, body)

    def emit(h, low, high):
        def body(r):
            stage[h, pl.ds(r, 64), :] = field[h, pl.ds(r + REACH - first, 64), :]
        sweep(low, high, 64, body)
        return pltpu.make_async_copy(
            stage.at[h, pl.ds(low, high - low)],
            out.at[pl.ds(low, high - low), pl.ds(h * LANES, LANES)],
            out_sem.at[h, 0 if low == 64 else (1 if low == 0 else 2)])

    reach = [offsets[k] for k in range(BANDS)]
    weight = [weights[k] for k in range(BANDS)]

    def band(h, low, high, upper=True, lower=True, up_from=None, up_to=None, down_from=None, down_to=None):
        n = 64

        def body(t):
            acc = jnp.zeros((n, LANES), jnp.float32)
            spot = lax.broadcasted_iota(jnp.int32, (n, LANES), 0)
            for k in range(BANDS):
                part = None
                if upper:
                    at = t + reach[k]
                    part = field[h, pl.ds(at, n), :]
                    if up_from is not None:
                        part = jnp.where(spot >= up_from + REACH - at, part, 0.0)
                    if up_to is not None:
                        part = jnp.where(spot < up_to + REACH - at, part, 0.0)
                if lower:
                    at = t - reach[k]
                    down = field[h, pl.ds(at, n), :]
                    if down_from is not None:
                        down = jnp.where(spot >= down_from + REACH - at, down, 0.0)
                    if down_to is not None:
                        down = jnp.where(spot < down_to + REACH - at, down, 0.0)
                    part = down if part is None else part + down
                acc = acc + weight[k] * part
            adj[h, pl.ds(t, n), :] = acc
        sweep(low + REACH, high + REACH, n, body)

    def backward(h, low, high, step):
        for l in reversed(range(LAYERS)):
            def body(q, l=l):
                if l == LAYERS - 1:
                    a = adj[h, pl.ds(2 * q + 1, step, stride=2), :]
                    b = adj[h, pl.ds(2 * q + 2, step, stride=2), :]
                elif l % 2 == 1:
                    a = xb[h, l, pl.ds(q, step), :]
                    b = xa[h, l, pl.ds(q + 1, step), :]
                else:
                    a = xb[h, l, pl.ds(q - 1, step), :]
                    b = xa[h, l, pl.ds(q, step), :]
                prod[h, l, pl.ds(q, step), :] = b * sa[h, l, pl.ds(q, step), :] - a * sb[h, l, pl.ds(q, step), :]
                if l > 0:
                    c = coef[l, pl.ds(q, step), :]
                    s = coef[LAYERS + l, pl.ds(q, step), :]
                    xa[h, l - 1, pl.ds(q, step), :] = c * a + s * b
                    xb[h, l - 1, pl.ds(q, step), :] = c * b - s * a
            sweep(low, high, step, body)

    outs = []
    for load in loads:
        load.wait()
    for h in range(halves):
        forward(h, q_own, q_end - 16, STEP)
        outs.append(emit(h, 64, rows - 64))
        outs[-1].start()
        band(h, REACH + 16, rows - REACH - 48)
        backward(h, q_own + 264, q_end - 280, STEP)

    for h in range(halves):
        for copy in halo_copies[h]:
            copy.wait()
        raw[h, 8:8 + SENT, :] = land[h, 0]
        raw[h, FRONT + rows:FRONT + rows + SENT, :] = land[h, 1]
        forward(h, q_lo, q_own + 8, STEP)
        forward(h, q_end - 24, q_hi, 40)
        for low, high in ((0, 64), (rows - 64, rows)):
            outs.append(emit(h, low, high))
            outs[-1].start()
        band(h, -HALF, 0, lower=False, up_from=0)
        band(h, 0, REACH + 64, down_from=-HALF)
        band(h, rows - REACH - 64, rows - HALF)
        band(h, rows - HALF, rows, up_to=rows)
        band(h, rows, rows + HALF, upper=False, down_to=rows - HALF)
        backward(h, q_lo, q_lo + 432, STEP)
        backward(h, q_hi - 432, q_hi, STEP)

    diagonal = (lax.broadcasted_iota(jnp.int32, (LANES, LANES), 0)
                == lax.broadcasted_iota(jnp.int32, (LANES, LANES), 1))

    def collapse(q):
        for l in range(LAYERS):
            x = prod[0, l, pl.ds(q, LANES), :]
            for h in range(1, halves):
                x = x + prod[h, l, pl.ds(q, LANES), :]
            s = jnp.sum(x, axis=1, keepdims=True)
            line = jnp.sum(jnp.where(diagonal, s, 0.0), axis=0, keepdims=True)
            window[l:l + 1, pl.ds(pl.multiple_of(q, LANES), LANES)] = line

    sweep(0, total_q, LANES, collapse)
    whole = window[...]
    rolled = pltpu.roll(whole, 1, 1)
    whole = jnp.where(jnp.logical_and(odd, moved), rolled, whole)[:LAYERS]
    mid = q_own + pairs // 2
    own_g[pl.ds(col, 1)] = jnp.concatenate([whole[:, q_own:mid], whole[:, mid:q_end]], 0)[None]
    send_l[...] = jnp.concatenate([whole[:, 0:LANES], whole[:, LANES:HALF]], 0)
    send_r[...] = jnp.concatenate([whole[:, q_end:q_end + LANES], whole[:, q_end + LANES:]], 0)
    copies = []
    for i, c in enumerate(others):
        copies.append(remote(own_g.at[col], own_g.at[col], o_send.at[i], o_recv.at[col], (blk, c)))
    for i, c in enumerate(every):
        copies.append(remote(send_l, right_g.at[col], l_send.at[i], l_recv.at[col], (before, c)))
        copies.append(remote(send_r, left_g.at[col], r_send.at[i], r_recv.at[col], (after, c)))
    for copy in copies:
        copy.start()
    for copy in copies:
        copy.wait_send()
    for i, c in enumerate(others):
        remote(own_g.at[c], own_g.at[c], o_send.at[i], o_recv.at[c], (blk, c)).wait_recv()
    for i, c in enumerate(every):
        remote(send_l, right_g.at[c], l_send.at[i], l_recv.at[c], (before, c)).wait_recv()
        remote(send_r, left_g.at[c], r_send.at[i], r_recv.at[c], (after, c)).wait_recv()
    own = own_g[0]
    left = left_g[0]
    right = right_g[0]
    for c in range(1, ncol):
        own = own + own_g[c]
        left = left + left_g[c]
        right = right + right_g[c]
    line = jnp.concatenate([own[:LAYERS], own[LAYERS:]], 1)
    line = jnp.concatenate([
        line[:, :LANES] + left[:LAYERS],
        line[:, LANES:HALF] + left[LAYERS:],
        line[:, HALF:pairs - HALF],
        line[:, pairs - HALF:pairs - LANES] + right[:LAYERS],
        line[:, pairs - LANES:] + right[LAYERS:],
    ], 1)
    grad[...] = line
    for copy in outs:
        copy.wait()


def on_device(nblk, ncol, slab, angles, pairing, band_offsets, band_weights):
    rows, width = slab.shape
    halves = width // LANES
    pairs = rows // 2
    total_q = pairs + REACH
    buf_q = total_q + 8
    f32 = jnp.float32
    dma = pltpu.SemaphoreType.DMA
    smem = pl.BlockSpec(memory_space=pltpu.SMEM)
    anywhere = pl.BlockSpec(memory_space=pl.ANY)
    return pl.pallas_call(
        functools.partial(kernel, nblk, ncol),
        out_shape=(
            jax.ShapeDtypeStruct((rows, width), f32),
            jax.ShapeDtypeStruct((LAYERS, pairs), f32),
        ),
        in_specs=[smem, smem, smem, anywhere, anywhere],
        out_specs=(anywhere, pl.BlockSpec(memory_space=pltpu.VMEM)),
        scratch_shapes=[
            pltpu.VMEM((halves, FRONT + rows + SENT + 16, LANES), f32),
            pltpu.VMEM((halves, 2, SENT, LANES), f32),
            pltpu.VMEM((LAYERS, total_q), f32),
            pltpu.VMEM((2 * LAYERS, total_q, LANES), f32),
            pltpu.VMEM((halves, LAYERS, buf_q, LANES), f32),
            pltpu.VMEM((halves, LAYERS, buf_q, LANES), f32),
            pltpu.VMEM((halves, rows + 2 * REACH + 16, LANES), f32),
            pltpu.VMEM((halves, rows + 2 * REACH + 16, LANES), f32),
            pltpu.VMEM((halves, LAYERS - 1, buf_q, LANES), f32),
            pltpu.VMEM((halves, LAYERS - 1, buf_q, LANES), f32),
            pltpu.VMEM((halves, LAYERS, total_q, LANES), f32),
            pltpu.VMEM((halves, rows, LANES), f32),
            pltpu.VMEM((2 * LAYERS, total_q), f32),
            pltpu.VMEM((ncol, 2 * LAYERS, pairs // 2), f32),
            pltpu.VMEM((ncol, 2 * LAYERS, LANES), f32),
            pltpu.VMEM((ncol, 2 * LAYERS, LANES), f32),
            pltpu.VMEM((2 * LAYERS, LANES), f32),
            pltpu.VMEM((2 * LAYERS, LANES), f32),
            dma((halves,)), dma, dma((halves, 3)),
            dma((halves, 2)), dma((halves, 2)),
            dma((2,)), dma((2,)),
            dma((ncol - 1,)), dma((ncol,)),
            dma((ncol,)), dma((ncol,)),
            dma((ncol,)), dma((ncol,)),
        ],
        compiler_params=pltpu.CompilerParams(
            collective_id=0, has_side_effects=True, vmem_limit_bytes=58 * 2**20),
    )(pairing, band_offsets, band_weights, slab, angles)


def solution(mesh):
    in_specs = (P("blk", "col"), P(None, "blk"), P(), P(), P())
    out_specs = (P("blk", "col"), P(None, "blk"))
    return jax.shard_map(
        functools.partial(on_device, mesh.shape["blk"], mesh.shape["col"]),
        mesh=mesh, in_specs=in_specs, out_specs=out_specs, check_vma=False,
    )
```

```python
import functools

import jax
import jax.numpy as jnp
from jax import lax
from jax.experimental import pallas as pl
from jax.experimental.pallas import tpu as pltpu
from jax.sharding import PartitionSpec as P

LAYERS = 4
BANDS = 8
REACH = 512
HALF = REACH // 2
SENT = HALF + 8
LANES = 128
FRONT = SENT + 8
MESH = pl.DeviceIdType.MESH


def sweep(low, high, step, body):
    assert (high - low) % step == 0 and low % 8 == 0 and step % 8 == 0
    if high - low == step:
        body(low)
        return

    def one(i, carry):
        body(pl.multiple_of(low + i * step, 8))
        return carry

    lax.fori_loop(0, (high - low) // step, one, 0)


def sin_cos(x):
    n = jnp.floor(x * 0.6366197723675814 + 0.5)
    r = ((x - n * 1.5703125) - n * 4.837512969970703e-4) - n * 7.54978995489188e-8
    z = r * r
    s = ((-1.9515295891e-4 * z + 8.3321608736e-3) * z - 1.6666654611e-1) * z * r + r
    c = ((2.443315711809948e-5 * z - 1.388731625493765e-3) * z + 4.166664568298827e-2) * z * z - 0.5 * z + 1.0
    odd = jnp.abs(n) == 1.0
    even_sign = jnp.where(n == 0.0, 1.0, -1.0)
    return jnp.where(odd, n * c, even_sign * s), jnp.where(odd, -n * s, even_sign * c)


def kernel(
    nblk, ncol,
    pairing, offsets, weights, slab, angles,
    out, grad,
    raw, far, angw, coef, sa, sb, field, left_f, right_f, cut, adj, xa, xb, prod, stage, window,
    own_g, left_g, right_g, send_l, send_r,
    load_sem, ang_sem, out_sem, n_send, n_recv, h_send, h_recv, a_send, a_recv,
    o_send, o_recv, l_send, l_recv, r_send, r_recv,
):
    rows, width = slab.shape
    halves = width // LANES
    pairs = rows // 2
    q_own = HALF
    q_end = q_own + pairs
    q_lo, q_hi = 120, q_end + 136
    total_q = pairs + REACH
    blk = lax.axis_index("blk")
    col = lax.axis_index("col")
    after = lax.rem(blk + 1, nblk)
    before = lax.rem(blk + nblk - 1, nblk)
    others = [lax.rem(col + d, ncol) for d in range(1, ncol)]
    every = [col] + others

    barrier = pltpu.get_barrier_semaphore()
    peers = [(blk, c) for c in others] + [(b, c) for b in (after, before) for c in every]
    for peer in peers:
        pl.semaphore_signal(barrier, inc=1, device_id=peer, device_id_type=MESH)

    loads = []
    for h in range(halves):
        loads.append(pltpu.make_async_copy(
            slab.at[:, pl.ds(h * LANES, LANES)], raw.at[h, pl.ds(FRONT, rows)], load_sem.at[h]))
    own_ang = pltpu.make_async_copy(angles, angw.at[:, pl.ds(HALF, pairs)], ang_sem)
    own_ang.start()
    for load in loads:
        load.start()

    def remote(src, dst, s, r, peer):
        return pltpu.make_async_remote_copy(
            src_ref=src, dst_ref=dst, send_sem=s, recv_sem=r, device_id=peer, device_id_type=MESH)

    ang_copies = [
        remote(angles.at[:, pl.ds(pairs - HALF, HALF)], angw.at[:, pl.ds(0, HALF)], a_send.at[0], a_recv.at[0], (after, col)),
        remote(angles.at[:, pl.ds(0, HALF)], angw.at[:, pl.ds(q_end, HALF)], a_send.at[1], a_recv.at[1], (before, col)),
    ]
    near_copies = []
    far_copies = []
    for h in range(halves):
        lanes = pl.ds(h * LANES, LANES)
        near_copies += [
            remote(slab.at[pl.ds(rows - 8, 8), lanes], raw.at[h, pl.ds(FRONT - 8, 8)], n_send.at[h, 0], n_recv.at[h, 0], (after, col)),
            remote(slab.at[pl.ds(0, 8), lanes], raw.at[h, pl.ds(FRONT + rows, 8)], n_send.at[h, 1], n_recv.at[h, 1], (before, col)),
        ]
        far_copies.append([
            remote(slab.at[pl.ds(rows - SENT, HALF), lanes], far.at[h, 0], h_send.at[h, 0], h_recv.at[h, 0], (after, col)),
            remote(slab.at[pl.ds(8, HALF), lanes], far.at[h, 1], h_send.at[h, 1], h_recv.at[h, 1], (before, col)),
        ])

    pl.semaphore_wait(barrier, len(peers))
    for copy in ang_copies + near_copies:
        copy.start()
    for pair in far_copies:
        for copy in pair:
            copy.start()

    first = pairing[0]

    def zeros(n):
        return jnp.zeros((n, LANES), jnp.float32)

    left_f[...] = zeros(left_f.shape[0])
    right_f[...] = zeros(right_f.shape[0])
    cut[...] = zeros(cut.shape[0])
    for h in range(halves):
        raw[h, 0:8, :] = zeros(8)
        raw[h, FRONT + rows + SENT:FRONT + rows + SENT + 16, :] = zeros(16)
        adj[h, 2 * q_lo:REACH - HALF, :] = zeros(REACH - HALF - 2 * q_lo)
        top = REACH + rows + HALF
        adj[h, top:2 * q_hi + 8, :] = zeros(2 * q_hi + 8 - top)
        field[h, 0:REACH, :] = zeros(REACH)
        field[h, REACH + rows:, :] = zeros(field.shape[1] - REACH - rows)
        for l in range(LAYERS):
            sa[h, l, q_hi:q_hi + 8, :] = zeros(8)
            sb[h, l, q_lo - 8:q_lo, :] = zeros(8)
        for l in range(LAYERS - 1):
            xb[h, l, q_lo - 8:q_lo, :] = zeros(8)
            xa[h, l, q_hi:q_hi + 8, :] = zeros(8)

    own_ang.wait()
    for copy in ang_copies:
        copy.wait()
    theta = angw[...]
    mid = total_q // 2
    sine, cosine = sin_cos(jnp.concatenate([theta[:, :mid], theta[:, mid:]], 0))
    both = jnp.concatenate([
        jnp.concatenate([cosine[:LAYERS], sine[:LAYERS]], 0),
        jnp.concatenate([cosine[LAYERS:], sine[LAYERS:]], 0)], 1)
    rolled = pltpu.roll(both, total_q - 1, 1)
    odd = lax.broadcasted_iota(jnp.int32, both.shape, 0) % 2 == 1
    moved = jnp.full(both.shape, first, jnp.int32) == 1
    window[...] = jnp.where(jnp.logical_and(odd, moved), rolled, both)

    def spread(q):
        part = window[:, pl.ds(pl.multiple_of(q, LANES), LANES)]
        turned = part.T
        for j in range(2 * LAYERS):
            coef[j, pl.ds(q, LANES), :] = jnp.broadcast_to(turned[:, j:j + 1], (LANES, LANES))

    sweep(0, total_q, LANES, spread)

    def held(h, l, q, n):
        if l == LAYERS - 1:
            return adj[h, pl.ds(2 * q + 1, n, stride=2), :], adj[h, pl.ds(2 * q + 2, n, stride=2), :]
        if l % 2 == 1:
            return xb[h, l, pl.ds(q, n), :], xa[h, l, pl.ds(q + 1, n), :]
        return xb[h, l, pl.ds(q - 1, n), :], xa[h, l, pl.ds(q, n), :]

    def forward(h, low, high, step, target, shift, products):
        for l in range(LAYERS):
            def body(q, l=l):
                if l == 0:
                    a = raw[h, pl.ds(2 * q - 2 * q_lo + first, step, stride=2), :]
                    b = raw[h, pl.ds(2 * q - 2 * q_lo + 1 + first, step, stride=2), :]
                elif l % 2 == 1:
                    a = sb[h, l - 1, pl.ds(q, step), :]
                    b = sa[h, l - 1, pl.ds(q + 1, step), :]
                else:
                    a = sb[h, l - 1, pl.ds(q - 1, step), :]
                    b = sa[h, l - 1, pl.ds(q, step), :]
                c = coef[l, pl.ds(q, step), :]
                s = coef[LAYERS + l, pl.ds(q, step), :]
                new_a = c * a - s * b
                new_b = s * a + c * b
                sa[h, l, pl.ds(q, step), :] = new_a
                sb[h, l, pl.ds(q, step), :] = new_b
                if products:
                    a, b = held(h, l, q, step)
                    prod[h, l, pl.ds(q, step), :] = b * new_a - a * new_b
                if l == LAYERS - 1:
                    target[pl.ds(2 * q + 1 - shift, step, stride=2), :] = new_a
                    target[pl.ds(2 * q + 2 - shift, step, stride=2), :] = new_b
            sweep(low, high, step, body)

    reach = [offsets[k] for k in range(BANDS)]
    weight = [weights[k] for k in range(BANDS)]

    def band(h, low, high, upper=None, lower=None, shift=0, more=False):
        n = 64

        def body(t):
            acc = adj[h, pl.ds(t, n), :] if more else None
            for k in range(BANDS):
                part = None
                if upper is not None:
                    part = upper[pl.ds(t - shift + reach[k], n), :]
                if lower is not None:
                    down = lower[pl.ds(t - shift - reach[k], n), :]
                    part = down if part is None else part + down
                part = weight[k] * part
                acc = part if acc is None else acc + part
            adj[h, pl.ds(t, n), :] = acc
        sweep(low + REACH, high + REACH, n, body)

    def backward(h, low, high, step, products):
        for l in reversed(range(LAYERS)):
            if l == 0 and not products:
                continue

            def body(q, l=l):
                a, b = held(h, l, q, step)
                if products:
                    prod[h, l, pl.ds(q, step), :] = b * sa[h, l, pl.ds(q, step), :] - a * sb[h, l, pl.ds(q, step), :]
                if l > 0:
                    c = coef[l, pl.ds(q, step), :]
                    s = coef[LAYERS + l, pl.ds(q, step), :]
                    xa[h, l - 1, pl.ds(q, step), :] = c * a + s * b
                    xb[h, l - 1, pl.ds(q, step), :] = c * b - s * a
            sweep(low, high, step, body)

    def collapse(q, n, more):
        start = q // LANES * LANES
        wanted = (lax.broadcasted_iota(jnp.int32, (n, LANES), 0) + (q - start)
                  == lax.broadcasted_iota(jnp.int32, (n, LANES), 1))
        for l in range(LAYERS):
            x = prod[0, l, q:q + n, :]
            for h in range(1, halves):
                x = x + prod[h, l, q:q + n, :]
            s = jnp.sum(x, axis=1, keepdims=True)
            line = jnp.sum(jnp.where(wanted, s, 0.0), axis=0, keepdims=True)
            if more:
                line = line + window[l:l + 1, start:start + LANES]
            window[l:l + 1, start:start + LANES] = line

    for load in loads:
        load.wait()
    for copy in near_copies:
        copy.wait()
    outs = []
    edge = REACH + rows
    for h in range(halves):
        forward(h, q_own - 8, q_end + 8, 104, field.at[h], 0, False)

        def emit(r, h=h):
            stage[h, pl.ds(r, 128), :] = field[h, pl.ds(r + REACH - first, 128), :]

        sweep(0, rows, 128, emit)
        outs.append(pltpu.make_async_copy(stage.at[h], out.at[:, pl.ds(h * LANES, LANES)], out_sem.at[h]))
        outs[-1].start()
        field[h, REACH - 16:REACH, :] = zeros(16)
        field[h, edge:edge + 24, :] = zeros(24)
        cut[0:HALF, :] = field[h, rows:rows + HALF, :]
        whole = field.at[h]
        band(h, -HALF, 0, upper=whole)
        band(h, 0, rows, upper=whole, lower=whole)
        band(h, rows, rows + HALF, lower=cut, shift=rows)
        backward(h, q_lo, q_own + 8, 144, False)
        backward(h, q_own + 248, q_end - 248, 176, True)
        backward(h, q_end - 136, q_hi, 136, True)
    collapse(q_own + 264, 120, False)
    for q in range(q_own + 384, q_end - 384, LANES):
        collapse(q, LANES, False)
    collapse(q_end - 384, 120, False)
    collapse(q_end - 120, 120, False)

    for h in range(halves):
        for copy in far_copies[h]:
            copy.wait()
        raw[h, 8:8 + HALF, :] = far[h, 0]
        raw[h, FRONT + rows + 8:FRONT + rows + SENT, :] = far[h, 1]
        forward(h, q_lo, q_own, 136, left_f, 0, True)
        forward(h, q_end - 8, q_hi, 144, right_f, rows, True)
        left_f[2 * q_lo:HALF, :] = zeros(HALF - 2 * q_lo)
        left_f[REACH:REACH + 8, :] = zeros(8)
        right_f[REACH - 16:REACH, :] = zeros(16)
        right_f[REACH + HALF:REACH + HALF + 24, :] = zeros(24)
        band(h, 0, REACH, lower=left_f, more=True)
        band(h, rows - REACH, rows - HALF, upper=right_f, shift=rows, more=True)
        backward(h, q_own - 8, q_own + 264, 136, True)
        backward(h, q_end - 264, q_end - 120, 144, True)
    collapse(q_lo, 8, False)
    collapse(LANES, LANES, False)
    collapse(q_own, LANES, False)
    collapse(q_own + LANES, LANES, False)
    collapse(q_own + HALF, 8, True)
    collapse(q_end - 264, 8, True)
    collapse(q_end - HALF, LANES, False)
    collapse(q_end - LANES, 8, True)
    collapse(q_end, LANES, False)
    collapse(q_end + LANES, 8, False)

    whole = window[...]
    rolled = pltpu.roll(whole, 1, 1)
    whole = jnp.where(jnp.logical_and(odd, moved), rolled, whole)[:LAYERS]
    mid = q_own + pairs // 2
    own_g[pl.ds(col, 1)] = jnp.concatenate([whole[:, q_own:mid], whole[:, mid:q_end]], 0)[None]
    send_l[...] = jnp.concatenate([whole[:, 0:LANES], whole[:, LANES:HALF]], 0)
    send_r[...] = jnp.concatenate([whole[:, q_end:q_end + LANES], whole[:, q_end + LANES:]], 0)
    copies = []
    for i, c in enumerate(others):
        copies.append(remote(own_g.at[col], own_g.at[col], o_send.at[i], o_recv.at[col], (blk, c)))
    for i, c in enumerate(every):
        copies.append(remote(send_l, right_g.at[col], l_send.at[i], l_recv.at[col], (before, c)))
        copies.append(remote(send_r, left_g.at[col], r_send.at[i], r_recv.at[col], (after, c)))
    for copy in copies:
        copy.start()
    for copy in copies:
        copy.wait_send()
    for i, c in enumerate(others):
        remote(own_g.at[c], own_g.at[c], o_send.at[i], o_recv.at[c], (blk, c)).wait_recv()
    for i, c in enumerate(every):
        remote(send_l, right_g.at[c], l_send.at[i], l_recv.at[c], (before, c)).wait_recv()
        remote(send_r, left_g.at[c], r_send.at[i], r_recv.at[c], (after, c)).wait_recv()
    own = own_g[0]
    left = left_g[0]
    right = right_g[0]
    for c in range(1, ncol):
        own = own + own_g[c]
        left = left + left_g[c]
        right = right + right_g[c]
    line = jnp.concatenate([own[:LAYERS], own[LAYERS:]], 1)
    line = jnp.concatenate([
        line[:, :LANES] + left[:LAYERS],
        line[:, LANES:HALF] + left[LAYERS:],
        line[:, HALF:pairs - HALF],
        line[:, pairs - HALF:pairs - LANES] + right[:LAYERS],
        line[:, pairs - LANES:] + right[LAYERS:],
    ], 1)
    grad[...] = line
    for copy in outs:
        copy.wait()


def on_device(nblk, ncol, slab, angles, pairing, band_offsets, band_weights):
    rows, width = slab.shape
    halves = width // LANES
    pairs = rows // 2
    total_q = pairs + REACH
    buf_q = total_q + 8
    f32 = jnp.float32
    dma = pltpu.SemaphoreType.DMA
    smem = pl.BlockSpec(memory_space=pltpu.SMEM)
    anywhere = pl.BlockSpec(memory_space=pl.ANY)
    return pl.pallas_call(
        functools.partial(kernel, nblk, ncol),
        out_shape=(
            jax.ShapeDtypeStruct((rows, width), f32),
            jax.ShapeDtypeStruct((LAYERS, pairs), f32),
        ),
        in_specs=[smem, smem, smem, anywhere, anywhere],
        out_specs=(anywhere, pl.BlockSpec(memory_space=pltpu.VMEM)),
        scratch_shapes=[
            pltpu.VMEM((halves, FRONT + rows + SENT + 16, LANES), f32),
            pltpu.VMEM((halves, 2, HALF, LANES), f32),
            pltpu.VMEM((LAYERS, total_q), f32),
            pltpu.VMEM((2 * LAYERS, total_q, LANES), f32),
            pltpu.VMEM((halves, LAYERS, buf_q, LANES), f32),
            pltpu.VMEM((halves, LAYERS, buf_q, LANES), f32),
            pltpu.VMEM((halves, rows + 2 * REACH + 16, LANES), f32),
            pltpu.VMEM((2 * REACH + 8, LANES), f32),
            pltpu.VMEM((REACH + HALF + 24, LANES), f32),
            pltpu.VMEM((REACH + HALF, LANES), f32),
            pltpu.VMEM((halves, rows + 2 * REACH + 16, LANES), f32),
            pltpu.VMEM((halves, LAYERS - 1, buf_q, LANES), f32),
            pltpu.VMEM((halves, LAYERS - 1, buf_q, LANES), f32),
            pltpu.VMEM((halves, LAYERS, total_q, LANES), f32),
            pltpu.VMEM((halves, rows, LANES), f32),
            pltpu.VMEM((2 * LAYERS, total_q), f32),
            pltpu.VMEM((ncol, 2 * LAYERS, pairs // 2), f32),
            pltpu.VMEM((ncol, 2 * LAYERS, LANES), f32),
            pltpu.VMEM((ncol, 2 * LAYERS, LANES), f32),
            pltpu.VMEM((2 * LAYERS, LANES), f32),
            pltpu.VMEM((2 * LAYERS, LANES), f32),
            dma((halves,)), dma, dma((halves,)),
            dma((halves, 2)), dma((halves, 2)),
            dma((halves, 2)), dma((halves, 2)),
            dma((2,)), dma((2,)),
            dma((ncol - 1,)), dma((ncol,)),
            dma((ncol,)), dma((ncol,)),
            dma((ncol,)), dma((ncol,)),
        ],
        compiler_params=pltpu.CompilerParams(
            collective_id=0, has_side_effects=True, vmem_limit_bytes=58 * 2**20),
    )(pairing, band_offsets, band_weights, slab, angles)


def solution(mesh):
    in_specs = (P("blk", "col"), P(None, "blk"), P(), P(), P())
    out_specs = (P("blk", "col"), P(None, "blk"))
    return jax.shard_map(
        functools.partial(on_device, mesh.shape["blk"], mesh.shape["col"]),
        mesh=mesh, in_specs=in_specs, out_specs=out_specs, check_vma=False,
    )
```

```python
import functools

import jax
import jax.numpy as jnp
from jax import lax
from jax.experimental import pallas as pl
from jax.experimental.pallas import tpu as pltpu
from jax.sharding import PartitionSpec as P

LAYERS = 4
BANDS = 8
REACH = 512
HALF = REACH // 2
SENT = HALF + 8
LANES = 128
FRONT = SENT + 8
MESH = pl.DeviceIdType.MESH


def sweep(low, high, step, body):
    assert (high - low) % step == 0 and low % 8 == 0 and step % 8 == 0
    if high - low == step:
        body(low)
        return

    def one(i, carry):
        body(pl.multiple_of(low + i * step, 8))
        return carry

    lax.fori_loop(0, (high - low) // step, one, 0)


def sin_cos(x):
    n = jnp.floor(x * 0.6366197723675814 + 0.5)
    r = ((x - n * 1.5703125) - n * 4.837512969970703e-4) - n * 7.54978995489188e-8
    z = r * r
    s = ((-1.9515295891e-4 * z + 8.3321608736e-3) * z - 1.6666654611e-1) * z * r + r
    c = ((2.443315711809948e-5 * z - 1.388731625493765e-3) * z + 4.166664568298827e-2) * z * z - 0.5 * z + 1.0
    odd = jnp.abs(n) == 1.0
    even_sign = jnp.where(n == 0.0, 1.0, -1.0)
    return jnp.where(odd, n * c, even_sign * s), jnp.where(odd, -n * s, even_sign * c)


def kernel(
    nblk, ncol,
    pairing, offsets, weights, slab, angles,
    out, grad,
    raw, far, angw, coef, sa, sb, field, left_f, right_f, cut, adj, xa, xb, prod, window,
    own_g, left_g, right_g, send_l, send_r,
    load_sem, ang_sem, n_send, n_recv, h_send, h_recv, a_send, a_recv,
    o_send, o_recv, l_send, l_recv, r_send, r_recv,
):
    rows, width = slab.shape
    halves = width // LANES
    pairs = rows // 2
    q_own = HALF
    q_end = q_own + pairs
    q_lo, q_hi = 120, q_end + 136
    total_q = pairs + REACH
    blk = lax.axis_index("blk")
    col = lax.axis_index("col")
    after = lax.rem(blk + 1, nblk)
    before = lax.rem(blk + nblk - 1, nblk)
    others = [lax.rem(col + d, ncol) for d in range(1, ncol)]
    every = [col] + others

    barrier = pltpu.get_barrier_semaphore()
    peers = [(blk, c) for c in others] + [(b, c) for b in (after, before) for c in every]
    for peer in peers:
        pl.semaphore_signal(barrier, inc=1, device_id=peer, device_id_type=MESH)

    loads = []
    for h in range(halves):
        loads.append(pltpu.make_async_copy(
            slab.at[:, pl.ds(h * LANES, LANES)], raw.at[h, pl.ds(FRONT, rows)], load_sem.at[h]))
    own_ang = pltpu.make_async_copy(angles, angw.at[:, pl.ds(HALF, pairs)], ang_sem)
    own_ang.start()
    for load in loads:
        load.start()

    def remote(src, dst, s, r, peer):
        return pltpu.make_async_remote_copy(
            src_ref=src, dst_ref=dst, send_sem=s, recv_sem=r, device_id=peer, device_id_type=MESH)

    ang_copies = [
        remote(angles.at[:, pl.ds(pairs - HALF, HALF)], angw.at[:, pl.ds(0, HALF)], a_send.at[0], a_recv.at[0], (after, col)),
        remote(angles.at[:, pl.ds(0, HALF)], angw.at[:, pl.ds(q_end, HALF)], a_send.at[1], a_recv.at[1], (before, col)),
    ]
    near_copies = []
    far_copies = []
    for h in range(halves):
        lanes = pl.ds(h * LANES, LANES)
        near_copies += [
            remote(slab.at[pl.ds(rows - 8, 8), lanes], raw.at[h, pl.ds(FRONT - 8, 8)], n_send.at[h, 0], n_recv.at[h, 0], (after, col)),
            remote(slab.at[pl.ds(0, 8), lanes], raw.at[h, pl.ds(FRONT + rows, 8)], n_send.at[h, 1], n_recv.at[h, 1], (before, col)),
        ]
        far_copies.append([
            remote(slab.at[pl.ds(rows - SENT, HALF), lanes], far.at[h, 0], h_send.at[h, 0], h_recv.at[h, 0], (after, col)),
            remote(slab.at[pl.ds(8, HALF), lanes], far.at[h, 1], h_send.at[h, 1], h_recv.at[h, 1], (before, col)),
        ])

    pl.semaphore_wait(barrier, len(peers))
    for copy in ang_copies + near_copies:
        copy.start()
    for pair in far_copies:
        for copy in pair:
            copy.start()

    first = pairing[0]

    def zeros(n):
        return jnp.zeros((n, LANES), jnp.float32)

    left_f[...] = zeros(left_f.shape[0])
    right_f[...] = zeros(right_f.shape[0])
    cut[...] = zeros(cut.shape[0])
    for h in range(halves):
        raw[h, 0:8, :] = zeros(8)
        raw[h, FRONT + rows + SENT:FRONT + rows + SENT + 16, :] = zeros(16)
        adj[h, 2 * q_lo:REACH - HALF, :] = zeros(REACH - HALF - 2 * q_lo)
        top = REACH + rows + HALF
        adj[h, top:2 * q_hi + 8, :] = zeros(2 * q_hi + 8 - top)
        field[h, 0:REACH, :] = zeros(REACH)
        field[h, REACH + rows:, :] = zeros(field.shape[1] - REACH - rows)
        for l in range(LAYERS):
            sa[h, l, q_hi:q_hi + 8, :] = zeros(8)
            sb[h, l, q_lo - 8:q_lo, :] = zeros(8)
        for l in range(LAYERS - 1):
            xb[h, l, q_lo - 8:q_lo, :] = zeros(8)
            xa[h, l, q_hi:q_hi + 8, :] = zeros(8)

    own_ang.wait()
    for copy in ang_copies:
        copy.wait()
    theta = angw[...]
    mid = total_q // 2
    sine, cosine = sin_cos(jnp.concatenate([theta[:, :mid], theta[:, mid:]], 0))
    both = jnp.concatenate([
        jnp.concatenate([cosine[:LAYERS], sine[:LAYERS]], 0),
        jnp.concatenate([cosine[LAYERS:], sine[LAYERS:]], 0)], 1)
    rolled = pltpu.roll(both, total_q - 1, 1)
    odd = lax.broadcasted_iota(jnp.int32, both.shape, 0) % 2 == 1
    moved = jnp.full(both.shape, first, jnp.int32) == 1
    window[...] = jnp.where(jnp.logical_and(odd, moved), rolled, both)

    def spread(q):
        part = window[:, pl.ds(pl.multiple_of(q, LANES), LANES)]
        turned = part.T
        for j in range(2 * LAYERS):
            coef[j, pl.ds(q, LANES), :] = jnp.broadcast_to(turned[:, j:j + 1], (LANES, LANES))

    sweep(0, total_q, LANES, spread)

    def held(h, l, q, n):
        if l == LAYERS - 1:
            return adj[h, pl.ds(2 * q + 1, n, stride=2), :], adj[h, pl.ds(2 * q + 2, n, stride=2), :]
        if l % 2 == 1:
            return xb[h, l, pl.ds(q, n), :], xa[h, l, pl.ds(q + 1, n), :]
        return xb[h, l, pl.ds(q - 1, n), :], xa[h, l, pl.ds(q, n), :]

    def forward(h, low, high, step, target, shift, products):
        for l in range(LAYERS):
            def body(q, l=l):
                if l == 0:
                    a = raw[h, pl.ds(2 * q - 2 * q_lo + first, step, stride=2), :]
                    b = raw[h, pl.ds(2 * q - 2 * q_lo + 1 + first, step, stride=2), :]
                elif l % 2 == 1:
                    a = sb[h, l - 1, pl.ds(q, step), :]
                    b = sa[h, l - 1, pl.ds(q + 1, step), :]
                else:
                    a = sb[h, l - 1, pl.ds(q - 1, step), :]
                    b = sa[h, l - 1, pl.ds(q, step), :]
                c = coef[l, pl.ds(q, step), :]
                s = coef[LAYERS + l, pl.ds(q, step), :]
                new_a = c * a - s * b
                new_b = s * a + c * b
                sa[h, l, pl.ds(q, step), :] = new_a
                sb[h, l, pl.ds(q, step), :] = new_b
                if products:
                    a, b = held(h, l, q, step)
                    prod[h, l, pl.ds(q, step), :] = b * new_a - a * new_b
                if l == LAYERS - 1:
                    target[pl.ds(2 * q + 1 - shift, step, stride=2), :] = new_a
                    target[pl.ds(2 * q + 2 - shift, step, stride=2), :] = new_b
            sweep(low, high, step, body)

    reach = [offsets[k] for k in range(BANDS)]
    weight = [weights[k] for k in range(BANDS)]

    def band(h, low, high, upper=None, lower=None, shift=0, more=False):
        n = 64

        def body(t):
            acc = adj[h, pl.ds(t, n), :] if more else None
            for k in range(BANDS):
                part = None
                if upper is not None:
                    part = upper[pl.ds(t - shift + reach[k], n), :]
                if lower is not None:
                    down = lower[pl.ds(t - shift - reach[k], n), :]
                    part = down if part is None else part + down
                part = weight[k] * part
                acc = part if acc is None else acc + part
            adj[h, pl.ds(t, n), :] = acc
        sweep(low + REACH, high + REACH, n, body)

    def backward(h, low, high, step, products):
        for l in reversed(range(LAYERS)):
            if l == 0 and not products:
                continue

            def body(q, l=l):
                a, b = held(h, l, q, step)
                if products:
                    prod[h, l, pl.ds(q, step), :] = b * sa[h, l, pl.ds(q, step), :] - a * sb[h, l, pl.ds(q, step), :]
                if l > 0:
                    c = coef[l, pl.ds(q, step), :]
                    s = coef[LAYERS + l, pl.ds(q, step), :]
                    xa[h, l - 1, pl.ds(q, step), :] = c * a + s * b
                    xb[h, l - 1, pl.ds(q, step), :] = c * b - s * a
            sweep(low, high, step, body)

    def collapse(q, n, more):
        start = q // LANES * LANES
        wanted = (lax.broadcasted_iota(jnp.int32, (n, LANES), 0) + (q - start)
                  == lax.broadcasted_iota(jnp.int32, (n, LANES), 1))
        for l in range(LAYERS):
            x = prod[0, l, q:q + n, :]
            for h in range(1, halves):
                x = x + prod[h, l, q:q + n, :]
            s = jnp.sum(x, axis=1, keepdims=True)
            line = jnp.sum(jnp.where(wanted, s, 0.0), axis=0, keepdims=True)
            if more:
                line = line + window[l:l + 1, start:start + LANES]
            window[l:l + 1, start:start + LANES] = line

    for load in loads:
        load.wait()
    for copy in near_copies:
        copy.wait()
    edge = REACH + rows
    for h in range(halves):
        forward(h, q_own - 8, q_end + 8, 104, field.at[h], 0, False)

        def emit(r, h=h):
            out[pl.ds(r, 128), h * LANES:(h + 1) * LANES] = field[h, pl.ds(r + REACH - first, 128), :]

        sweep(0, rows, 128, emit)
        field[h, REACH - 16:REACH, :] = zeros(16)
        field[h, edge:edge + 24, :] = zeros(24)
        cut[0:HALF, :] = field[h, rows:rows + HALF, :]
        whole = field.at[h]
        band(h, -HALF, 0, upper=whole)
        band(h, 0, rows, upper=whole, lower=whole)
        band(h, rows, rows + HALF, lower=cut, shift=rows)
        backward(h, q_lo, q_own + 8, 144, False)
        backward(h, q_own + 248, q_end - 248, 176, True)
        backward(h, q_end - 136, q_hi, 136, True)
    collapse(q_own + 264, 120, False)
    for q in range(q_own + 384, q_end - 384, LANES):
        collapse(q, LANES, False)
    collapse(q_end - 384, 120, False)
    collapse(q_end - 120, 120, False)

    for h in range(halves):
        for copy in far_copies[h]:
            copy.wait()
        raw[h, 8:8 + HALF, :] = far[h, 0]
        raw[h, FRONT + rows + 8:FRONT + rows + SENT, :] = far[h, 1]
        forward(h, q_lo, q_own, 136, left_f, 0, True)
        forward(h, q_end - 8, q_hi, 144, right_f, rows, True)
        left_f[2 * q_lo:HALF, :] = zeros(HALF - 2 * q_lo)
        left_f[REACH:REACH + 8, :] = zeros(8)
        right_f[REACH - 16:REACH, :] = zeros(16)
        right_f[REACH + HALF:REACH + HALF + 24, :] = zeros(24)
        band(h, 0, REACH, lower=left_f, more=True)
        band(h, rows - REACH, rows - HALF, upper=right_f, shift=rows, more=True)
        backward(h, q_own - 8, q_own + 264, 136, True)
        backward(h, q_end - 264, q_end - 120, 144, True)
    collapse(q_lo, 8, False)
    collapse(LANES, LANES, False)
    collapse(q_own, LANES, False)
    collapse(q_own + LANES, LANES, False)
    collapse(q_own + HALF, 8, True)
    collapse(q_end - 264, 8, True)
    collapse(q_end - HALF, LANES, False)
    collapse(q_end - LANES, 8, True)
    collapse(q_end, LANES, False)
    collapse(q_end + LANES, 8, False)

    whole = window[...]
    rolled = pltpu.roll(whole, 1, 1)
    whole = jnp.where(jnp.logical_and(odd, moved), rolled, whole)[:LAYERS]
    mid = q_own + pairs // 2
    own_g[pl.ds(col, 1)] = jnp.concatenate([whole[:, q_own:mid], whole[:, mid:q_end]], 0)[None]
    send_l[...] = jnp.concatenate([whole[:, 0:LANES], whole[:, LANES:HALF]], 0)
    send_r[...] = jnp.concatenate([whole[:, q_end:q_end + LANES], whole[:, q_end + LANES:]], 0)
    copies = []
    for i, c in enumerate(others):
        copies.append(remote(own_g.at[col], own_g.at[col], o_send.at[i], o_recv.at[col], (blk, c)))
    for i, c in enumerate(every):
        copies.append(remote(send_l, right_g.at[col], l_send.at[i], l_recv.at[col], (before, c)))
        copies.append(remote(send_r, left_g.at[col], r_send.at[i], r_recv.at[col], (after, c)))
    for copy in copies:
        copy.start()
    for copy in copies:
        copy.wait_send()
    for i, c in enumerate(others):
        remote(own_g.at[c], own_g.at[c], o_send.at[i], o_recv.at[c], (blk, c)).wait_recv()
    for i, c in enumerate(every):
        remote(send_l, right_g.at[c], l_send.at[i], l_recv.at[c], (before, c)).wait_recv()
        remote(send_r, left_g.at[c], r_send.at[i], r_recv.at[c], (after, c)).wait_recv()
    own = own_g[0]
    left = left_g[0]
    right = right_g[0]
    for c in range(1, ncol):
        own = own + own_g[c]
        left = left + left_g[c]
        right = right + right_g[c]
    line = jnp.concatenate([own[:LAYERS], own[LAYERS:]], 1)
    line = jnp.concatenate([
        line[:, :LANES] + left[:LAYERS],
        line[:, LANES:HALF] + left[LAYERS:],
        line[:, HALF:pairs - HALF],
        line[:, pairs - HALF:pairs - LANES] + right[:LAYERS],
        line[:, pairs - LANES:] + right[LAYERS:],
    ], 1)
    grad[...] = line


def hand_out(evolved, gradient, evolved_out, gradient_out, sems):
    copies = [
        pltpu.make_async_copy(evolved, evolved_out, sems.at[0]),
        pltpu.make_async_copy(gradient, gradient_out, sems.at[1]),
    ]
    for copy in copies:
        copy.start()
    for copy in copies:
        copy.wait()


def on_device(nblk, ncol, slab, angles, pairing, band_offsets, band_weights):
    rows, width = slab.shape
    halves = width // LANES
    pairs = rows // 2
    total_q = pairs + REACH
    buf_q = total_q + 8
    f32 = jnp.float32
    dma = pltpu.SemaphoreType.DMA
    smem = pl.BlockSpec(memory_space=pltpu.SMEM)
    anywhere = pl.BlockSpec(memory_space=pl.ANY)
    evolved, gradient = pl.pallas_call(
        functools.partial(kernel, nblk, ncol),
        out_shape=(
            pltpu.VMEM((rows, width), f32),
            pltpu.VMEM((LAYERS, pairs), f32),
        ),
        in_specs=[smem, smem, smem, anywhere, anywhere],
        out_specs=(pl.BlockSpec(memory_space=pltpu.VMEM), pl.BlockSpec(memory_space=pltpu.VMEM)),
        scratch_shapes=[
            pltpu.VMEM((halves, FRONT + rows + SENT + 16, LANES), f32),
            pltpu.VMEM((halves, 2, HALF, LANES), f32),
            pltpu.VMEM((LAYERS, total_q), f32),
            pltpu.VMEM((2 * LAYERS, total_q, LANES), f32),
            pltpu.VMEM((halves, LAYERS, buf_q, LANES), f32),
            pltpu.VMEM((halves, LAYERS, buf_q, LANES), f32),
            pltpu.VMEM((halves, rows + 2 * REACH + 16, LANES), f32),
            pltpu.VMEM((2 * REACH + 8, LANES), f32),
            pltpu.VMEM((REACH + HALF + 24, LANES), f32),
            pltpu.VMEM((REACH + HALF, LANES), f32),
            pltpu.VMEM((halves, rows + 2 * REACH + 16, LANES), f32),
            pltpu.VMEM((halves, LAYERS - 1, buf_q, LANES), f32),
            pltpu.VMEM((halves, LAYERS - 1, buf_q, LANES), f32),
            pltpu.VMEM((halves, LAYERS, total_q, LANES), f32),
            pltpu.VMEM((2 * LAYERS, total_q), f32),
            pltpu.VMEM((ncol, 2 * LAYERS, pairs // 2), f32),
            pltpu.VMEM((ncol, 2 * LAYERS, LANES), f32),
            pltpu.VMEM((ncol, 2 * LAYERS, LANES), f32),
            pltpu.VMEM((2 * LAYERS, LANES), f32),
            pltpu.VMEM((2 * LAYERS, LANES), f32),
            dma((halves,)), dma,
            dma((halves, 2)), dma((halves, 2)),
            dma((halves, 2)), dma((halves, 2)),
            dma((2,)), dma((2,)),
            dma((ncol - 1,)), dma((ncol,)),
            dma((ncol,)), dma((ncol,)),
            dma((ncol,)), dma((ncol,)),
        ],
        compiler_params=pltpu.CompilerParams(
            collective_id=0, has_side_effects=True, vmem_limit_bytes=58 * 2**20),
    )(pairing, band_offsets, band_weights, slab, angles)
    return pl.pallas_call(
        hand_out,
        out_shape=(
            jax.ShapeDtypeStruct((rows, width), f32),
            jax.ShapeDtypeStruct((LAYERS, pairs), f32),
        ),
        in_specs=[pl.BlockSpec(memory_space=pltpu.VMEM)] * 2,
        out_specs=(anywhere, anywhere),
        scratch_shapes=[dma((2,))],
    )(evolved, gradient)


def solution(mesh):
    in_specs = (P("blk", "col"), P(None, "blk"), P(), P(), P())
    out_specs = (P("blk", "col"), P(None, "blk"))
    return jax.shard_map(
        functools.partial(on_device, mesh.shape["blk"], mesh.shape["col"]),
        mesh=mesh, in_specs=in_specs, out_specs=out_specs, check_vma=False,
    )
```

```python
import functools

import jax
import jax.numpy as jnp
from jax import lax
from jax.experimental import pallas as pl
from jax.experimental.pallas import tpu as pltpu
from jax.sharding import PartitionSpec as P

LAYERS = 4
BANDS = 8
REACH = 512
HALF = REACH // 2
SENT = HALF + 8
LANES = 128
FRONT = SENT + 8
MESH = pl.DeviceIdType.MESH


def sweep(low, high, step, body):
    assert (high - low) % step == 0 and low % 8 == 0 and step % 8 == 0
    if high - low == step:
        body(low)
        return

    def one(i, carry):
        body(pl.multiple_of(low + i * step, 8))
        return carry

    lax.fori_loop(0, (high - low) // step, one, 0)


def sin_cos(x):
    n = jnp.floor(x * 0.6366197723675814 + 0.5)
    r = ((x - n * 1.5703125) - n * 4.837512969970703e-4) - n * 7.54978995489188e-8
    z = r * r
    s = ((-1.9515295891e-4 * z + 8.3321608736e-3) * z - 1.6666654611e-1) * z * r + r
    c = ((2.443315711809948e-5 * z - 1.388731625493765e-3) * z + 4.166664568298827e-2) * z * z - 0.5 * z + 1.0
    odd = jnp.abs(n) == 1.0
    even_sign = jnp.where(n == 0.0, 1.0, -1.0)
    return jnp.where(odd, n * c, even_sign * s), jnp.where(odd, -n * s, even_sign * c)


def kernel(
    nblk, ncol,
    pairing, offsets, weights, slab, angles,
    out, grad,
    raw, far, angw, coef, sa, sb, field, left_f, right_f, cut, adj, xa, xb, prod, window,
    own_g, left_g, right_g, send_l, send_r,
    load_sem, ang_sem, n_send, n_recv, h_send, h_recv, a_send, a_recv,
    o_send, o_recv, l_send, l_recv, r_send, r_recv,
):
    rows, width = slab.shape
    halves = width // LANES
    pairs = rows // 2
    q_own = HALF
    q_end = q_own + pairs
    q_lo, q_hi = 120, q_end + 136
    total_q = pairs + REACH
    blk = lax.axis_index("blk")
    col = lax.axis_index("col")
    after = lax.rem(blk + 1, nblk)
    before = lax.rem(blk + nblk - 1, nblk)
    others = [lax.rem(col + d, ncol) for d in range(1, ncol)]
    every = [col] + others

    barrier = pltpu.get_barrier_semaphore()
    peers = [(blk, c) for c in others] + [(b, c) for b in (after, before) for c in every]
    for peer in peers:
        pl.semaphore_signal(barrier, inc=1, device_id=peer, device_id_type=MESH)

    loads = []
    for h in range(halves):
        loads.append(pltpu.make_async_copy(
            slab.at[:, pl.ds(h * LANES, LANES)], raw.at[h, pl.ds(FRONT, rows)], load_sem.at[h]))
    own_ang = pltpu.make_async_copy(angles, angw.at[:, pl.ds(HALF, pairs)], ang_sem)
    own_ang.start()
    for load in loads:
        load.start()

    def remote(src, dst, s, r, peer):
        return pltpu.make_async_remote_copy(
            src_ref=src, dst_ref=dst, send_sem=s, recv_sem=r, device_id=peer, device_id_type=MESH)

    ang_copies = [
        remote(angles.at[:, pl.ds(pairs - HALF, HALF)], angw.at[:, pl.ds(0, HALF)], a_send.at[0], a_recv.at[0], (after, col)),
        remote(angles.at[:, pl.ds(0, HALF)], angw.at[:, pl.ds(q_end, HALF)], a_send.at[1], a_recv.at[1], (before, col)),
    ]
    near_copies = []
    far_copies = []
    for h in range(halves):
        lanes = pl.ds(h * LANES, LANES)
        near_copies += [
            remote(slab.at[pl.ds(rows - 8, 8), lanes], raw.at[h, pl.ds(FRONT - 8, 8)], n_send.at[h, 0], n_recv.at[h, 0], (after, col)),
            remote(slab.at[pl.ds(0, 8), lanes], raw.at[h, pl.ds(FRONT + rows, 8)], n_send.at[h, 1], n_recv.at[h, 1], (before, col)),
        ]
        far_copies.append([
            remote(slab.at[pl.ds(rows - SENT, HALF), lanes], far.at[h, 0], h_send.at[h, 0], h_recv.at[h, 0], (after, col)),
            remote(slab.at[pl.ds(8, HALF), lanes], far.at[h, 1], h_send.at[h, 1], h_recv.at[h, 1], (before, col)),
        ])

    pl.semaphore_wait(barrier, len(peers))
    for copy in ang_copies + near_copies:
        copy.start()
    for pair in far_copies:
        for copy in pair:
            copy.start()

    first = pairing[0]

    def zeros(n):
        return jnp.zeros((n, LANES), jnp.float32)

    left_f[...] = zeros(left_f.shape[0])
    right_f[...] = zeros(right_f.shape[0])
    cut[...] = zeros(cut.shape[0])
    for h in range(halves):
        raw[h, 0:8, :] = zeros(8)
        raw[h, FRONT + rows + SENT:FRONT + rows + SENT + 16, :] = zeros(16)
        adj[h, 2 * q_lo:REACH - HALF, :] = zeros(REACH - HALF - 2 * q_lo)
        top = REACH + rows + HALF
        adj[h, top:2 * q_hi + 8, :] = zeros(2 * q_hi + 8 - top)
        field[h, 0:REACH, :] = zeros(REACH)
        field[h, REACH + rows:, :] = zeros(field.shape[1] - REACH - rows)
        for l in range(LAYERS - 1):
            sa[h, l, q_hi:q_hi + 8, :] = zeros(8)
            sb[h, l, q_lo - 8:q_lo, :] = zeros(8)
            xb[h, l, q_lo - 8:q_lo, :] = zeros(8)
            xa[h, l, q_hi:q_hi + 8, :] = zeros(8)

    def coefficients(theta):
        mid = theta.shape[1] // 2
        sine, cosine = sin_cos(jnp.concatenate([theta[:, :mid], theta[:, mid:]], 0))
        return jnp.concatenate([
            jnp.concatenate([cosine[:LAYERS], sine[:LAYERS]], 0),
            jnp.concatenate([cosine[LAYERS:], sine[LAYERS:]], 0)], 1)

    def aligned(both):
        rolled = pltpu.roll(both, both.shape[1] - 1, 1)
        odd = lax.broadcasted_iota(jnp.int32, both.shape, 0) % 2 == 1
        moved = jnp.full(both.shape, first, jnp.int32) == 1
        return jnp.where(jnp.logical_and(odd, moved), rolled, both)

    def spread(q):
        turned = window[:, q:q + LANES].T
        for j in range(2 * LAYERS):
            coef[j, q:q + LANES, :] = jnp.broadcast_to(turned[:, j:j + 1], (LANES, LANES))

    own_ang.wait()
    own_both = coefficients(angw[:, q_own:q_end])
    window[:, q_own:q_end] = aligned(own_both)
    for q in range(q_own, q_end - LANES, LANES):
        spread(q)
    for copy in ang_copies:
        copy.wait()
    left_both = coefficients(angw[:, :q_own])
    right_both = coefficients(angw[:, q_end:])
    window[...] = aligned(jnp.concatenate([left_both, own_both, right_both], 1))
    for q in (0, LANES, q_end - LANES, q_end, q_end + LANES):
        spread(q)

    def held(h, l, q, n):
        if l == LAYERS - 1:
            return adj[h, pl.ds(2 * q + 1, n, stride=2), :], adj[h, pl.ds(2 * q + 2, n, stride=2), :]
        if l % 2 == 1:
            return xb[h, l, pl.ds(q, n), :], xa[h, l, pl.ds(q + 1, n), :]
        return xb[h, l, pl.ds(q - 1, n), :], xa[h, l, pl.ds(q, n), :]

    def forward(h, low, high, step, target, shift, products):
        for l in range(LAYERS):
            def body(q, l=l):
                if l == 0:
                    a = raw[h, pl.ds(2 * q - 2 * q_lo + first, step, stride=2), :]
                    b = raw[h, pl.ds(2 * q - 2 * q_lo + 1 + first, step, stride=2), :]
                elif l % 2 == 1:
                    a = sb[h, l - 1, pl.ds(q, step), :]
                    b = sa[h, l - 1, pl.ds(q + 1, step), :]
                else:
                    a = sb[h, l - 1, pl.ds(q - 1, step), :]
                    b = sa[h, l - 1, pl.ds(q, step), :]
                c = coef[l, pl.ds(q, step), :]
                s = coef[LAYERS + l, pl.ds(q, step), :]
                new_a = c * a - s * b
                new_b = s * a + c * b
                if l < LAYERS - 1:
                    sa[h, l, pl.ds(q, step), :] = new_a
                    sb[h, l, pl.ds(q, step), :] = new_b
                if products:
                    a, b = held(h, l, q, step)
                    prod[h, l, pl.ds(q, step), :] = b * new_a - a * new_b
                if l == LAYERS - 1:
                    target[pl.ds(2 * q + 1 - shift, step, stride=2), :] = new_a
                    target[pl.ds(2 * q + 2 - shift, step, stride=2), :] = new_b
            sweep(low, high, step, body)

    reach = [offsets[k] for k in range(BANDS)]
    weight = [weights[k] for k in range(BANDS)]

    def band(h, low, high, upper=None, lower=None, shift=0, more=False):
        n = 128

        def body(t):
            acc = adj[h, pl.ds(t, n), :] if more else None
            for k in range(BANDS):
                part = None
                if upper is not None:
                    part = upper[pl.ds(t - shift + reach[k], n), :]
                if lower is not None:
                    down = lower[pl.ds(t - shift - reach[k], n), :]
                    part = down if part is None else part + down
                part = weight[k] * part
                acc = part if acc is None else acc + part
            adj[h, pl.ds(t, n), :] = acc
        sweep(low + REACH, high + REACH, n, body)

    def backward(h, low, high, step, products):
        for l in reversed(range(LAYERS)):
            if l == 0 and not products:
                continue

            def body(q, l=l):
                a, b = held(h, l, q, step)
                if l > 0:
                    c = coef[l, pl.ds(q, step), :]
                    s = coef[LAYERS + l, pl.ds(q, step), :]
                    new_a = c * a + s * b
                    new_b = c * b - s * a
                    xa[h, l - 1, pl.ds(q, step), :] = new_a
                    xb[h, l - 1, pl.ds(q, step), :] = new_b
                if products and l % 2 == 0:
                    prod[h, l, pl.ds(q, step), :] = b * sa[h, l, pl.ds(q, step), :] - a * sb[h, l, pl.ds(q, step), :]
                elif products:
                    prod[h, l, pl.ds(q, step), :] = (
                        new_b * sb[h, l - 1, pl.ds(q, step), :] - new_a * sa[h, l - 1, pl.ds(q + 1, step), :])
            sweep(low, high, step, body)

    def collapse(q, n, more):
        start = q // LANES * LANES
        wanted = (lax.broadcasted_iota(jnp.int32, (n, LANES), 0) + (q - start)
                  == lax.broadcasted_iota(jnp.int32, (n, LANES), 1))
        for l in range(LAYERS):
            x = prod[0, l, q:q + n, :]
            for h in range(1, halves):
                x = x + prod[h, l, q:q + n, :]
            s = jnp.sum(x, axis=1, keepdims=True)
            line = jnp.sum(jnp.where(wanted, s, 0.0), axis=0, keepdims=True)
            if more:
                line = line + window[l:l + 1, start:start + LANES]
            window[l:l + 1, start:start + LANES] = line

    for load in loads:
        load.wait()
    for copy in near_copies:
        copy.wait()
    edge = REACH + rows
    for h in range(halves):
        forward(h, q_own - 8, q_end + 8, 104, field.at[h], 0, False)

        def emit(r, h=h):
            out[pl.ds(r, 128), h * LANES:(h + 1) * LANES] = field[h, pl.ds(r + REACH - first, 128), :]

        sweep(0, rows, 128, emit)
        field[h, REACH - 16:REACH, :] = zeros(16)
        field[h, edge:edge + 24, :] = zeros(24)
        cut[0:HALF, :] = field[h, rows:rows + HALF, :]
        whole = field.at[h]
        band(h, -HALF, 0, upper=whole)
        band(h, 0, rows, upper=whole, lower=whole)
        band(h, rows, rows + HALF, lower=cut, shift=rows)
        backward(h, q_lo, q_own + 8, 144, False)
        backward(h, q_own + 248, q_end - 248, 176, True)
        backward(h, q_end - 136, q_hi, 136, True)
    collapse(q_own + 264, 120, False)
    for q in range(q_own + 384, q_end - 384, LANES):
        collapse(q, LANES, False)
    collapse(q_end - 384, 120, False)
    collapse(q_end - 120, 120, False)

    for h in range(halves):
        for copy in far_copies[h]:
            copy.wait()
        raw[h, 8:8 + HALF, :] = far[h, 0]
        raw[h, FRONT + rows + 8:FRONT + rows + SENT, :] = far[h, 1]
        forward(h, q_lo, q_own, 136, left_f, 0, True)
        forward(h, q_end - 8, q_hi, 144, right_f, rows, True)
        left_f[2 * q_lo:HALF, :] = zeros(HALF - 2 * q_lo)
        left_f[REACH:REACH + 8, :] = zeros(8)
        right_f[REACH - 16:REACH, :] = zeros(16)
        right_f[REACH + HALF:REACH + HALF + 24, :] = zeros(24)
        band(h, 0, REACH, lower=left_f, more=True)
        band(h, rows - REACH, rows - HALF, upper=right_f, shift=rows, more=True)
        backward(h, q_own - 8, q_own + 264, 136, True)
        backward(h, q_end - 264, q_end - 120, 144, True)
    collapse(q_lo, 8, False)
    collapse(LANES, LANES, False)
    collapse(q_own, LANES, False)
    collapse(q_own + LANES, LANES, False)
    collapse(q_own + HALF, 8, True)
    collapse(q_end - 264, 8, True)
    collapse(q_end - HALF, LANES, False)
    collapse(q_end - LANES, 8, True)
    collapse(q_end, LANES, False)
    collapse(q_end + LANES, 8, False)

    whole = window[...]
    rolled = pltpu.roll(whole, 1, 1)
    odd = lax.broadcasted_iota(jnp.int32, whole.shape, 0) % 2 == 1
    moved = jnp.full(whole.shape, first, jnp.int32) == 1
    whole = jnp.where(jnp.logical_and(odd, moved), rolled, whole)[:LAYERS]
    mid = q_own + pairs // 2
    own_g[pl.ds(col, 1)] = jnp.concatenate([whole[:, q_own:mid], whole[:, mid:q_end]], 0)[None]
    send_l[...] = jnp.concatenate([whole[:, 0:LANES], whole[:, LANES:HALF]], 0)
    send_r[...] = jnp.concatenate([whole[:, q_end:q_end + LANES], whole[:, q_end + LANES:]], 0)
    copies = []
    for i, c in enumerate(others):
        copies.append(remote(own_g.at[col], own_g.at[col], o_send.at[i], o_recv.at[col], (blk, c)))
    for i, c in enumerate(every):
        copies.append(remote(send_l, right_g.at[col], l_send.at[i], l_recv.at[col], (before, c)))
        copies.append(remote(send_r, left_g.at[col], r_send.at[i], r_recv.at[col], (after, c)))
    for copy in copies:
        copy.start()
    for copy in copies:
        copy.wait_send()
    for i, c in enumerate(others):
        remote(own_g.at[c], own_g.at[c], o_send.at[i], o_recv.at[c], (blk, c)).wait_recv()
    for i, c in enumerate(every):
        remote(send_l, right_g.at[c], l_send.at[i], l_recv.at[c], (before, c)).wait_recv()
        remote(send_r, left_g.at[c], r_send.at[i], r_recv.at[c], (after, c)).wait_recv()
    own = own_g[0]
    left = left_g[0]
    right = right_g[0]
    for c in range(1, ncol):
        own = own + own_g[c]
        left = left + left_g[c]
        right = right + right_g[c]
    line = jnp.concatenate([own[:LAYERS], own[LAYERS:]], 1)
    line = jnp.concatenate([
        line[:, :LANES] + left[:LAYERS],
        line[:, LANES:HALF] + left[LAYERS:],
        line[:, HALF:pairs - HALF],
        line[:, pairs - HALF:pairs - LANES] + right[:LAYERS],
        line[:, pairs - LANES:] + right[LAYERS:],
    ], 1)
    grad[...] = line


def on_device(nblk, ncol, slab, angles, pairing, band_offsets, band_weights):
    rows, width = slab.shape
    halves = width // LANES
    pairs = rows // 2
    total_q = pairs + REACH
    buf_q = total_q + 8
    f32 = jnp.float32
    dma = pltpu.SemaphoreType.DMA
    smem = pl.BlockSpec(memory_space=pltpu.SMEM)
    anywhere = pl.BlockSpec(memory_space=pl.ANY)
    return pl.pallas_call(
        functools.partial(kernel, nblk, ncol),
        out_shape=(
            pltpu.VMEM((rows, width), f32),
            pltpu.VMEM((LAYERS, pairs), f32),
        ),
        in_specs=[smem, smem, smem, anywhere, anywhere],
        out_specs=(pl.BlockSpec(memory_space=pltpu.VMEM), pl.BlockSpec(memory_space=pltpu.VMEM)),
        scratch_shapes=[
            pltpu.VMEM((halves, FRONT + rows + SENT + 16, LANES), f32),
            pltpu.VMEM((halves, 2, HALF, LANES), f32),
            pltpu.VMEM((LAYERS, total_q), f32),
            pltpu.VMEM((2 * LAYERS, total_q, LANES), f32),
            pltpu.VMEM((halves, LAYERS - 1, buf_q, LANES), f32),
            pltpu.VMEM((halves, LAYERS - 1, buf_q, LANES), f32),
            pltpu.VMEM((halves, rows + 2 * REACH + 16, LANES), f32),
            pltpu.VMEM((2 * REACH + 8, LANES), f32),
            pltpu.VMEM((REACH + HALF + 24, LANES), f32),
            pltpu.VMEM((REACH + HALF, LANES), f32),
            pltpu.VMEM((halves, rows + 2 * REACH + 16, LANES), f32),
            pltpu.VMEM((halves, LAYERS - 1, buf_q, LANES), f32),
            pltpu.VMEM((halves, LAYERS - 1, buf_q, LANES), f32),
            pltpu.VMEM((halves, LAYERS, total_q, LANES), f32),
            pltpu.VMEM((2 * LAYERS, total_q), f32),
            pltpu.VMEM((ncol, 2 * LAYERS, pairs // 2), f32),
            pltpu.VMEM((ncol, 2 * LAYERS, LANES), f32),
            pltpu.VMEM((ncol, 2 * LAYERS, LANES), f32),
            pltpu.VMEM((2 * LAYERS, LANES), f32),
            pltpu.VMEM((2 * LAYERS, LANES), f32),
            dma((halves,)), dma,
            dma((halves, 2)), dma((halves, 2)),
            dma((halves, 2)), dma((halves, 2)),
            dma((2,)), dma((2,)),
            dma((ncol - 1,)), dma((ncol,)),
            dma((ncol,)), dma((ncol,)),
            dma((ncol,)), dma((ncol,)),
        ],
        compiler_params=pltpu.CompilerParams(
            collective_id=0, has_side_effects=True, vmem_limit_bytes=58 * 2**20),
    )(pairing, band_offsets, band_weights, slab, angles)


def solution(mesh):
    in_specs = (P("blk", "col"), P(None, "blk"), P(), P(), P())
    out_specs = (P("blk", "col"), P(None, "blk"))
    return jax.shard_map(
        functools.partial(on_device, mesh.shape["blk"], mesh.shape["col"]),
        mesh=mesh, in_specs=in_specs, out_specs=out_specs, check_vma=False,
    )
```

```python
import functools

import jax
import jax.numpy as jnp
from jax import lax
from jax.experimental import pallas as pl
from jax.experimental.pallas import tpu as pltpu
from jax.sharding import PartitionSpec as P

LAYERS = 4
BANDS = 8
REACH = 512
HALF = REACH // 2
SENT = HALF + 8
LANES = 128
FRONT = SENT + 8
MESH = pl.DeviceIdType.MESH


def sweep(low, high, step, body):
    assert (high - low) % step == 0 and low % 8 == 0 and step % 8 == 0
    if high - low == step:
        body(low)
        return

    def one(i, carry):
        body(pl.multiple_of(low + i * step, 8))
        return carry

    lax.fori_loop(0, (high - low) // step, one, 0)


def sin_cos(x):
    n = jnp.floor(x * 0.6366197723675814 + 0.5)
    r = ((x - n * 1.5703125) - n * 4.837512969970703e-4) - n * 7.54978995489188e-8
    z = r * r
    s = ((-1.9515295891e-4 * z + 8.3321608736e-3) * z - 1.6666654611e-1) * z * r + r
    c = ((2.443315711809948e-5 * z - 1.388731625493765e-3) * z + 4.166664568298827e-2) * z * z - 0.5 * z + 1.0
    odd = jnp.abs(n) == 1.0
    even_sign = jnp.where(n == 0.0, 1.0, -1.0)
    return jnp.where(odd, n * c, even_sign * s), jnp.where(odd, -n * s, even_sign * c)


def kernel(
    nblk, ncol,
    pairing, offsets, weights, slab, angles,
    out, grad,
    raw, far, angw, coef, sa, sb, field, left_f, right_f, cut, adj, xa, xb, prod, window,
    own_g, left_g, right_g, send_l, send_r,
    load_sem, ang_sem, n_send, n_recv, h_send, h_recv, a_send, a_recv,
    o_send, o_recv, l_send, l_recv, r_send, r_recv,
):
    rows, width = slab.shape
    halves = width // LANES
    pairs = rows // 2
    q_own = HALF
    q_end = q_own + pairs
    q_lo, q_hi = 120, q_end + 136
    total_q = pairs + REACH
    blk = lax.axis_index("blk")
    col = lax.axis_index("col")
    after = lax.rem(blk + 1, nblk)
    before = lax.rem(blk + nblk - 1, nblk)
    others = [lax.rem(col + d, ncol) for d in range(1, ncol)]
    every = [col] + others

    barrier = pltpu.get_barrier_semaphore()
    peers = [(blk, c) for c in others] + [(b, c) for b in (after, before) for c in every]
    for peer in peers:
        pl.semaphore_signal(barrier, inc=1, device_id=peer, device_id_type=MESH)

    loads = []
    for h in range(halves):
        loads.append(pltpu.make_async_copy(
            slab.at[:, pl.ds(h * LANES, LANES)], raw.at[h, pl.ds(FRONT, rows)], load_sem.at[h]))
    own_ang = pltpu.make_async_copy(angles, angw.at[:, pl.ds(HALF, pairs)], ang_sem)
    own_ang.start()
    for load in loads:
        load.start()

    def remote(src, dst, s, r, peer):
        return pltpu.make_async_remote_copy(
            src_ref=src, dst_ref=dst, send_sem=s, recv_sem=r, device_id=peer, device_id_type=MESH)

    ang_copies = [
        remote(angles.at[:, pl.ds(pairs - HALF, HALF)], angw.at[:, pl.ds(0, HALF)], a_send.at[0], a_recv.at[0], (after, col)),
        remote(angles.at[:, pl.ds(0, HALF)], angw.at[:, pl.ds(q_end, HALF)], a_send.at[1], a_recv.at[1], (before, col)),
    ]
    near_copies = []
    far_copies = []
    for h in range(halves):
        lanes = pl.ds(h * LANES, LANES)
        near_copies += [
            remote(slab.at[pl.ds(rows - 8, 8), lanes], raw.at[h, pl.ds(FRONT - 8, 8)], n_send.at[h, 0], n_recv.at[h, 0], (after, col)),
            remote(slab.at[pl.ds(0, 8), lanes], raw.at[h, pl.ds(FRONT + rows, 8)], n_send.at[h, 1], n_recv.at[h, 1], (before, col)),
        ]
        far_copies.append([
            remote(slab.at[pl.ds(rows - SENT, HALF), lanes], far.at[h, 0], h_send.at[h, 0], h_recv.at[h, 0], (after, col)),
            remote(slab.at[pl.ds(8, HALF), lanes], far.at[h, 1], h_send.at[h, 1], h_recv.at[h, 1], (before, col)),
        ])

    first = pairing[0]

    def zeros(n):
        return jnp.zeros((n, LANES), jnp.float32)

    left_f[...] = zeros(left_f.shape[0])
    right_f[...] = zeros(right_f.shape[0])
    cut[...] = zeros(cut.shape[0])
    for h in range(halves):
        raw[h, 0:8, :] = zeros(8)
        raw[h, FRONT + rows + SENT:FRONT + rows + SENT + 16, :] = zeros(16)
        adj[h, 2 * q_lo:REACH - HALF, :] = zeros(REACH - HALF - 2 * q_lo)
        top = REACH + rows + HALF
        adj[h, top:2 * q_hi + 8, :] = zeros(2 * q_hi + 8 - top)
        field[h, 0:REACH, :] = zeros(REACH)
        field[h, REACH + rows:, :] = zeros(field.shape[1] - REACH - rows)
        for l in range(LAYERS - 1):
            sa[h, l, q_hi:q_hi + 8, :] = zeros(8)
            sb[h, l, q_lo - 8:q_lo, :] = zeros(8)
            xb[h, l, q_lo - 8:q_lo, :] = zeros(8)
            xa[h, l, q_hi:q_hi + 8, :] = zeros(8)

    def coefficients(theta):
        mid = theta.shape[1] // 2
        sine, cosine = sin_cos(jnp.concatenate([theta[:, :mid], theta[:, mid:]], 0))
        return jnp.concatenate([
            jnp.concatenate([cosine[:LAYERS], sine[:LAYERS]], 0),
            jnp.concatenate([cosine[LAYERS:], sine[LAYERS:]], 0)], 1)

    def aligned(both):
        rolled = pltpu.roll(both, both.shape[1] - 1, 1)
        odd = lax.broadcasted_iota(jnp.int32, both.shape, 0) % 2 == 1
        moved = jnp.full(both.shape, first, jnp.int32) == 1
        return jnp.where(jnp.logical_and(odd, moved), rolled, both)

    def spread(q, low=0, n=LANES):
        turned = window[:, q:q + LANES].T[low:low + n]
        for j in range(2 * LAYERS):
            coef[j, q + low:q + low + n, :] = jnp.broadcast_to(turned[:, j:j + 1], (n, LANES))

    own_ang.wait()
    own_both = coefficients(angw[:, q_own:q_end])
    window[:, q_own:q_end] = aligned(own_both)
    for q in range(q_own, q_end - LANES, LANES):
        spread(q)

    pl.semaphore_wait(barrier, len(peers))
    for copy in ang_copies + near_copies:
        copy.start()
    for pair in far_copies:
        for copy in pair:
            copy.start()

    for copy in ang_copies:
        copy.wait()
    left_both = coefficients(angw[:, :q_own])
    right_both = coefficients(angw[:, q_end:])
    window[...] = aligned(jnp.concatenate([left_both, own_both, right_both], 1))
    spread(0, q_lo, 8)
    for q in (LANES, q_end - LANES, q_end):
        spread(q)
    spread(q_end + LANES, 0, 8)

    def held(h, l, q, n):
        if l == LAYERS - 1:
            return adj[h, pl.ds(2 * q + 1, n, stride=2), :], adj[h, pl.ds(2 * q + 2, n, stride=2), :]
        if l % 2 == 1:
            return xb[h, l, pl.ds(q, n), :], xa[h, l, pl.ds(q + 1, n), :]
        return xb[h, l, pl.ds(q - 1, n), :], xa[h, l, pl.ds(q, n), :]

    def forward(halves_in, low, high, step, target, shift, products):
        for l in range(LAYERS):
            def body(q, l=l):
                c = coef[l, pl.ds(q, step), :]
                s = coef[LAYERS + l, pl.ds(q, step), :]
                for h in halves_in:
                    if l == 0:
                        a = raw[h, pl.ds(2 * q - 2 * q_lo + first, step, stride=2), :]
                        b = raw[h, pl.ds(2 * q - 2 * q_lo + 1 + first, step, stride=2), :]
                    elif l % 2 == 1:
                        a = sb[h, l - 1, pl.ds(q, step), :]
                        b = sa[h, l - 1, pl.ds(q + 1, step), :]
                    else:
                        a = sb[h, l - 1, pl.ds(q - 1, step), :]
                        b = sa[h, l - 1, pl.ds(q, step), :]
                    new_a = c * a - s * b
                    new_b = s * a + c * b
                    if l < LAYERS - 1:
                        sa[h, l, pl.ds(q, step), :] = new_a
                        sb[h, l, pl.ds(q, step), :] = new_b
                    if products:
                        a, b = held(h, l, q, step)
                        prod[h, l, pl.ds(q, step), :] = b * new_a - a * new_b
                    if l == LAYERS - 1:
                        into = target(h)
                        into[pl.ds(2 * q + 1 - shift, step, stride=2), :] = new_a
                        into[pl.ds(2 * q + 2 - shift, step, stride=2), :] = new_b
            sweep(low, high, step, body)

    reach = [offsets[k] for k in range(BANDS)]
    weight = [weights[k] for k in range(BANDS)]

    def band(h, low, high, upper=None, lower=None, shift=0, more=False):
        n = 128

        def body(t):
            acc = adj[h, pl.ds(t, n), :] if more else None
            for k in range(BANDS):
                part = None
                if upper is not None:
                    part = upper[pl.ds(t - shift + reach[k], n), :]
                if lower is not None:
                    down = lower[pl.ds(t - shift - reach[k], n), :]
                    part = down if part is None else part + down
                part = weight[k] * part
                acc = part if acc is None else acc + part
            adj[h, pl.ds(t, n), :] = acc
        sweep(low + REACH, high + REACH, n, body)

    def backward(halves_in, low, high, step, products):
        for l in reversed(range(LAYERS)):
            if l == 0 and not products:
                continue

            def body(q, l=l):
                if l > 0:
                    c = coef[l, pl.ds(q, step), :]
                    s = coef[LAYERS + l, pl.ds(q, step), :]
                for h in halves_in:
                    a, b = held(h, l, q, step)
                    if l > 0:
                        new_a = c * a + s * b
                        new_b = c * b - s * a
                        xa[h, l - 1, pl.ds(q, step), :] = new_a
                        xb[h, l - 1, pl.ds(q, step), :] = new_b
                    if products and l % 2 == 0:
                        prod[h, l, pl.ds(q, step), :] = b * sa[h, l, pl.ds(q, step), :] - a * sb[h, l, pl.ds(q, step), :]
                    elif products:
                        prod[h, l, pl.ds(q, step), :] = (
                            new_b * sb[h, l - 1, pl.ds(q, step), :] - new_a * sa[h, l - 1, pl.ds(q + 1, step), :])
            sweep(low, high, step, body)

    def collapse(q, n, more):
        start = q // LANES * LANES
        wanted = (lax.broadcasted_iota(jnp.int32, (n, LANES), 0) + (q - start)
                  == lax.broadcasted_iota(jnp.int32, (n, LANES), 1))
        for l in range(LAYERS):
            x = prod[0, l, q:q + n, :]
            for h in range(1, halves):
                x = x + prod[h, l, q:q + n, :]
            s = jnp.sum(x, axis=1, keepdims=True)
            line = jnp.sum(jnp.where(wanted, s, 0.0), axis=0, keepdims=True)
            if more:
                line = line + window[l:l + 1, start:start + LANES]
            window[l:l + 1, start:start + LANES] = line

    for load in loads:
        load.wait()
    for copy in near_copies:
        copy.wait()
    edge = REACH + rows
    both_halves = range(halves)
    forward(both_halves, q_own - 8, q_end + 8, 104, lambda h: field.at[h], 0, False)

    def emit(r):
        for h in both_halves:
            out[pl.ds(r, 128), h * LANES:(h + 1) * LANES] = field[h, pl.ds(r + REACH - first, 128), :]

    sweep(0, rows, 128, emit)
    for h in both_halves:
        field[h, REACH - 16:REACH, :] = zeros(16)
        field[h, edge:edge + 24, :] = zeros(24)
        cut[0:HALF, :] = field[h, rows:rows + HALF, :]
        whole = field.at[h]
        band(h, -HALF, 0, upper=whole)
        band(h, 0, rows, upper=whole, lower=whole)
        band(h, rows, rows + HALF, lower=cut, shift=rows)
    backward(both_halves, q_lo, q_own + 8, 72, False)
    backward(both_halves, q_own + 248, q_end - 248, 88, True)
    backward(both_halves, q_end - 136, q_hi, 136, True)
    collapse(q_own + 264, 120, False)
    for q in range(q_own + 384, q_end - 384, LANES):
        collapse(q, LANES, False)
    collapse(q_end - 384, 120, False)
    collapse(q_end - 120, 120, False)

    for h in range(halves):
        for copy in far_copies[h]:
            copy.wait()
        raw[h, 8:8 + HALF, :] = far[h, 0]
        raw[h, FRONT + rows + 8:FRONT + rows + SENT, :] = far[h, 1]
        forward([h], q_lo, q_own, 136, lambda h: left_f, 0, True)
        forward([h], q_end - 8, q_hi, 144, lambda h: right_f, rows, True)
        left_f[2 * q_lo:HALF, :] = zeros(HALF - 2 * q_lo)
        left_f[REACH:REACH + 8, :] = zeros(8)
        right_f[REACH - 16:REACH, :] = zeros(16)
        right_f[REACH + HALF:REACH + HALF + 24, :] = zeros(24)
        band(h, 0, REACH, lower=left_f, more=True)
        band(h, rows - REACH, rows - HALF, upper=right_f, shift=rows, more=True)
        backward([h], q_own - 8, q_own + 264, 136, True)
        backward([h], q_end - 264, q_end - 120, 144, True)
    collapse(q_lo, 8, False)
    collapse(LANES, LANES, False)
    collapse(q_own, LANES, False)
    collapse(q_own + LANES, LANES, False)
    collapse(q_own + HALF, 8, True)
    collapse(q_end - 264, 8, True)
    collapse(q_end - HALF, LANES, False)
    collapse(q_end - LANES, 8, True)
    collapse(q_end, LANES, False)
    collapse(q_end + LANES, 8, False)

    whole = window[...]
    rolled = pltpu.roll(whole, 1, 1)
    odd = lax.broadcasted_iota(jnp.int32, whole.shape, 0) % 2 == 1
    moved = jnp.full(whole.shape, first, jnp.int32) == 1
    whole = jnp.where(jnp.logical_and(odd, moved), rolled, whole)[:LAYERS]
    mid = q_own + pairs // 2
    own_g[pl.ds(col, 1)] = jnp.concatenate([whole[:, q_own:mid], whole[:, mid:q_end]], 0)[None]
    send_l[...] = jnp.concatenate([whole[:, 0:LANES], whole[:, LANES:HALF]], 0)
    send_r[...] = jnp.concatenate([whole[:, q_end:q_end + LANES], whole[:, q_end + LANES:]], 0)
    copies = []
    for i, c in enumerate(others):
        copies.append(remote(own_g.at[col], own_g.at[col], o_send.at[i], o_recv.at[col], (blk, c)))
    for i, c in enumerate(every):
        copies.append(remote(send_l, right_g.at[col], l_send.at[i], l_recv.at[col], (before, c)))
        copies.append(remote(send_r, left_g.at[col], r_send.at[i], r_recv.at[col], (after, c)))
    for copy in copies:
        copy.start()
    for copy in copies:
        copy.wait_send()
    for i, c in enumerate(others):
        remote(own_g.at[c], own_g.at[c], o_send.at[i], o_recv.at[c], (blk, c)).wait_recv()
    for i, c in enumerate(every):
        remote(send_l, right_g.at[c], l_send.at[i], l_recv.at[c], (before, c)).wait_recv()
        remote(send_r, left_g.at[c], r_send.at[i], r_recv.at[c], (after, c)).wait_recv()
    own = own_g[0]
    left = left_g[0]
    right = right_g[0]
    for c in range(1, ncol):
        own = own + own_g[c]
        left = left + left_g[c]
        right = right + right_g[c]
    line = jnp.concatenate([own[:LAYERS], own[LAYERS:]], 1)
    line = jnp.concatenate([
        line[:, :LANES] + left[:LAYERS],
        line[:, LANES:HALF] + left[LAYERS:],
        line[:, HALF:pairs - HALF],
        line[:, pairs - HALF:pairs - LANES] + right[:LAYERS],
        line[:, pairs - LANES:] + right[LAYERS:],
    ], 1)
    grad[...] = line


def on_device(nblk, ncol, slab, angles, pairing, band_offsets, band_weights):
    rows, width = slab.shape
    halves = width // LANES
    pairs = rows // 2
    total_q = pairs + REACH
    buf_q = total_q + 8
    f32 = jnp.float32
    dma = pltpu.SemaphoreType.DMA
    smem = pl.BlockSpec(memory_space=pltpu.SMEM)
    anywhere = pl.BlockSpec(memory_space=pl.ANY)
    return pl.pallas_call(
        functools.partial(kernel, nblk, ncol),
        out_shape=(
            pltpu.VMEM((rows, width), f32),
            pltpu.VMEM((LAYERS, pairs), f32),
        ),
        in_specs=[smem, smem, smem, anywhere, anywhere],
        out_specs=(pl.BlockSpec(memory_space=pltpu.VMEM), pl.BlockSpec(memory_space=pltpu.VMEM)),
        scratch_shapes=[
            pltpu.VMEM((halves, FRONT + rows + SENT + 16, LANES), f32),
            pltpu.VMEM((halves, 2, HALF, LANES), f32),
            pltpu.VMEM((LAYERS, total_q), f32),
            pltpu.VMEM((2 * LAYERS, total_q, LANES), f32),
            pltpu.VMEM((halves, LAYERS - 1, buf_q, LANES), f32),
            pltpu.VMEM((halves, LAYERS - 1, buf_q, LANES), f32),
            pltpu.VMEM((halves, rows + 2 * REACH + 16, LANES), f32),
            pltpu.VMEM((2 * REACH + 8, LANES), f32),
            pltpu.VMEM((REACH + HALF + 24, LANES), f32),
            pltpu.VMEM((REACH + HALF, LANES), f32),
            pltpu.VMEM((halves, rows + 2 * REACH + 16, LANES), f32),
            pltpu.VMEM((halves, LAYERS - 1, buf_q, LANES), f32),
            pltpu.VMEM((halves, LAYERS - 1, buf_q, LANES), f32),
            pltpu.VMEM((halves, LAYERS, total_q, LANES), f32),
            pltpu.VMEM((2 * LAYERS, total_q), f32),
            pltpu.VMEM((ncol, 2 * LAYERS, pairs // 2), f32),
            pltpu.VMEM((ncol, 2 * LAYERS, LANES), f32),
            pltpu.VMEM((ncol, 2 * LAYERS, LANES), f32),
            pltpu.VMEM((2 * LAYERS, LANES), f32),
            pltpu.VMEM((2 * LAYERS, LANES), f32),
            dma((halves,)), dma,
            dma((halves, 2)), dma((halves, 2)),
            dma((halves, 2)), dma((halves, 2)),
            dma((2,)), dma((2,)),
            dma((ncol - 1,)), dma((ncol,)),
            dma((ncol,)), dma((ncol,)),
            dma((ncol,)), dma((ncol,)),
        ],
        compiler_params=pltpu.CompilerParams(
            collective_id=0, has_side_effects=True, vmem_limit_bytes=58 * 2**20),
    )(pairing, band_offsets, band_weights, slab, angles)


def solution(mesh):
    in_specs = (P("blk", "col"), P(None, "blk"), P(), P(), P())
    out_specs = (P("blk", "col"), P(None, "blk"))
    return jax.shard_map(
        functools.partial(on_device, mesh.shape["blk"], mesh.shape["col"]),
        mesh=mesh, in_specs=in_specs, out_specs=out_specs, check_vma=False,
    )
```

```python
import functools

import jax
import jax.numpy as jnp
from jax import lax
from jax.experimental import pallas as pl
from jax.experimental.pallas import tpu as pltpu
from jax.sharding import PartitionSpec as P

LAYERS = 4
BANDS = 8
REACH = 512
HALF = REACH // 2
SENT = HALF + 8
LANES = 128
FRONT = SENT + 8
MESH = pl.DeviceIdType.MESH


def sweep(low, high, step, body):
    assert (high - low) % step == 0 and low % 8 == 0 and step % 8 == 0
    if high - low == step:
        body(low)
        return

    def one(i, carry):
        body(pl.multiple_of(low + i * step, 8))
        return carry

    lax.fori_loop(0, (high - low) // step, one, 0)


def sin_cos(x):
    n = jnp.floor(x * 0.6366197723675814 + 0.5)
    r = ((x - n * 1.5703125) - n * 4.837512969970703e-4) - n * 7.54978995489188e-8
    z = r * r
    s = ((-1.9515295891e-4 * z + 8.3321608736e-3) * z - 1.6666654611e-1) * z * r + r
    c = ((2.443315711809948e-5 * z - 1.388731625493765e-3) * z + 4.166664568298827e-2) * z * z - 0.5 * z + 1.0
    odd = jnp.abs(n) == 1.0
    even_sign = jnp.where(n == 0.0, 1.0, -1.0)
    return jnp.where(odd, n * c, even_sign * s), jnp.where(odd, -n * s, even_sign * c)


def kernel(
    nblk, ncol,
    pairing, offsets, weights, slab, angles,
    out, grad,
    raw, far, angw, coef, sa, sb, field, left_f, right_f, cut, adj, xa, xb, prod, window,
    own_g, left_g, right_g, send_l, send_r,
    load_sem, ang_sem, n_send, n_recv, h_send, h_recv, a_send, a_recv,
    o_send, o_recv, l_send, l_recv, r_send, r_recv,
):
    rows, width = slab.shape
    halves = width // LANES
    pairs = rows // 2
    q_own = HALF
    q_end = q_own + pairs
    q_lo, q_hi = 120, q_end + 136
    total_q = pairs + REACH
    blk = lax.axis_index("blk")
    col = lax.axis_index("col")
    after = lax.rem(blk + 1, nblk)
    before = lax.rem(blk + nblk - 1, nblk)
    others = [lax.rem(col + d, ncol) for d in range(1, ncol)]
    every = [col] + others

    barrier = pltpu.get_barrier_semaphore()
    peers = [(blk, c) for c in others] + [(b, c) for b in (after, before) for c in every]
    for peer in peers:
        pl.semaphore_signal(barrier, inc=1, device_id=peer, device_id_type=MESH)

    loads = []
    for h in range(halves):
        loads.append(pltpu.make_async_copy(
            slab.at[:, pl.ds(h * LANES, LANES)], raw.at[h, pl.ds(FRONT, rows)], load_sem.at[h]))
    own_ang = pltpu.make_async_copy(angles, angw.at[:, pl.ds(HALF, pairs)], ang_sem)
    own_ang.start()
    for load in loads:
        load.start()

    def remote(src, dst, s, r, peer):
        return pltpu.make_async_remote_copy(
            src_ref=src, dst_ref=dst, send_sem=s, recv_sem=r, device_id=peer, device_id_type=MESH)

    ang_copies = [
        remote(angles.at[:, pl.ds(pairs - HALF, HALF)], angw.at[:, pl.ds(0, HALF)], a_send.at[0], a_recv.at[0], (after, col)),
        remote(angles.at[:, pl.ds(0, HALF)], angw.at[:, pl.ds(q_end, HALF)], a_send.at[1], a_recv.at[1], (before, col)),
    ]
    near_copies = []
    far_copies = []
    for h in range(halves):
        lanes = pl.ds(h * LANES, LANES)
        near_copies += [
            remote(slab.at[pl.ds(rows - 8, 8), lanes], raw.at[h, pl.ds(FRONT - 8, 8)], n_send.at[h, 0], n_recv.at[h, 0], (after, col)),
            remote(slab.at[pl.ds(0, 8), lanes], raw.at[h, pl.ds(FRONT + rows, 8)], n_send.at[h, 1], n_recv.at[h, 1], (before, col)),
        ]
        far_copies.append([
            remote(slab.at[pl.ds(rows - SENT, HALF), lanes], far.at[h, 0], h_send.at[h, 0], h_recv.at[h, 0], (after, col)),
            remote(slab.at[pl.ds(8, HALF), lanes], far.at[h, 1], h_send.at[h, 1], h_recv.at[h, 1], (before, col)),
        ])

    first = pairing[0]

    def coefficients(theta):
        mid = theta.shape[1] // 2
        sine, cosine = sin_cos(jnp.concatenate([theta[:, :mid], theta[:, mid:]], 0))
        return jnp.concatenate([
            jnp.concatenate([cosine[:LAYERS], sine[:LAYERS]], 0),
            jnp.concatenate([cosine[LAYERS:], sine[LAYERS:]], 0)], 1)

    def aligned(both):
        rolled = pltpu.roll(both, both.shape[1] - 1, 1)
        odd = lax.broadcasted_iota(jnp.int32, both.shape, 0) % 2 == 1
        moved = jnp.full(both.shape, first, jnp.int32) == 1
        return jnp.where(jnp.logical_and(odd, moved), rolled, both)

    def spread(q, low=0, n=LANES):
        turned = window[:, q:q + LANES].T[low:low + n]
        for j in range(2 * LAYERS):
            coef[j, q + low:q + low + n, :] = jnp.broadcast_to(turned[:, j:j + 1], (n, LANES))

    own_ang.wait()
    own_both = coefficients(angw[:, q_own:q_end])
    window[:, q_own:q_end] = aligned(own_both)
    for q in range(q_own, q_end - LANES, LANES):
        spread(q)

    pl.semaphore_wait(barrier, len(peers))
    for copy in ang_copies + near_copies + far_copies[0]:
        copy.start()

    def zeros(n):
        return jnp.zeros((n, LANES), jnp.float32)

    left_f[...] = zeros(left_f.shape[0])
    right_f[...] = zeros(right_f.shape[0])
    cut[...] = zeros(cut.shape[0])
    for h in range(halves):
        raw[h, 0:8, :] = zeros(8)
        raw[h, FRONT + rows + SENT:FRONT + rows + SENT + 16, :] = zeros(16)
        adj[h, 2 * q_lo:REACH - HALF, :] = zeros(REACH - HALF - 2 * q_lo)
        top = REACH + rows + HALF
        adj[h, top:2 * q_hi + 8, :] = zeros(2 * q_hi + 8 - top)
        field[h, 0:REACH, :] = zeros(REACH)
        field[h, REACH + rows:, :] = zeros(field.shape[1] - REACH - rows)
        for l in range(LAYERS - 1):
            sa[h, l, q_hi:q_hi + 8, :] = zeros(8)
            sb[h, l, q_lo - 8:q_lo, :] = zeros(8)
            xb[h, l, q_lo - 8:q_lo, :] = zeros(8)
            xa[h, l, q_hi:q_hi + 8, :] = zeros(8)

    for copy in ang_copies:
        copy.wait()
    left_both = coefficients(angw[:, :q_own])
    right_both = coefficients(angw[:, q_end:])
    window[...] = aligned(jnp.concatenate([left_both, own_both, right_both], 1))
    spread(0, q_lo, 8)
    for q in (LANES, q_end - LANES, q_end):
        spread(q)
    spread(q_end + LANES, 0, 8)

    def held(h, l, q, n):
        if l == LAYERS - 1:
            return adj[h, pl.ds(2 * q + 1, n, stride=2), :], adj[h, pl.ds(2 * q + 2, n, stride=2), :]
        if l % 2 == 1:
            return xb[h, l, pl.ds(q, n), :], xa[h, l, pl.ds(q + 1, n), :]
        return xb[h, l, pl.ds(q - 1, n), :], xa[h, l, pl.ds(q, n), :]

    def forward(halves_in, low, high, step, target, shift, products):
        for l in range(LAYERS):
            def body(q, l=l):
                c = coef[l, pl.ds(q, step), :]
                s = coef[LAYERS + l, pl.ds(q, step), :]
                for h in halves_in:
                    if l == 0:
                        a = raw[h, pl.ds(2 * q - 2 * q_lo + first, step, stride=2), :]
                        b = raw[h, pl.ds(2 * q - 2 * q_lo + 1 + first, step, stride=2), :]
                    elif l % 2 == 1:
                        a = sb[h, l - 1, pl.ds(q, step), :]
                        b = sa[h, l - 1, pl.ds(q + 1, step), :]
                    else:
                        a = sb[h, l - 1, pl.ds(q - 1, step), :]
                        b = sa[h, l - 1, pl.ds(q, step), :]
                    new_a = c * a - s * b
                    new_b = s * a + c * b
                    if l < LAYERS - 1:
                        sa[h, l, pl.ds(q, step), :] = new_a
                        sb[h, l, pl.ds(q, step), :] = new_b
                    if products:
                        a, b = held(h, l, q, step)
                        prod[h, l, pl.ds(q, step), :] = b * new_a - a * new_b
                    if l == LAYERS - 1:
                        into = target(h)
                        into[pl.ds(2 * q + 1 - shift, step, stride=2), :] = new_a
                        into[pl.ds(2 * q + 2 - shift, step, stride=2), :] = new_b
            sweep(low, high, step, body)

    reach = [offsets[k] for k in range(BANDS)]
    weight = [weights[k] for k in range(BANDS)]

    def band(h, low, high, upper=None, lower=None, shift=0, more=False):
        n = 128

        def body(t):
            acc = adj[h, pl.ds(t, n), :] if more else None
            for k in range(BANDS):
                part = None
                if upper is not None:
                    part = upper[pl.ds(t - shift + reach[k], n), :]
                if lower is not None:
                    down = lower[pl.ds(t - shift - reach[k], n), :]
                    part = down if part is None else part + down
                part = weight[k] * part
                acc = part if acc is None else acc + part
            adj[h, pl.ds(t, n), :] = acc
        sweep(low + REACH, high + REACH, n, body)

    def backward(halves_in, low, high, step, products):
        for l in reversed(range(LAYERS)):
            if l == 0 and not products:
                continue

            def body(q, l=l):
                if l > 0:
                    c = coef[l, pl.ds(q, step), :]
                    s = coef[LAYERS + l, pl.ds(q, step), :]
                for h in halves_in:
                    a, b = held(h, l, q, step)
                    if l > 0:
                        new_a = c * a + s * b
                        new_b = c * b - s * a
                        xa[h, l - 1, pl.ds(q, step), :] = new_a
                        xb[h, l - 1, pl.ds(q, step), :] = new_b
                    if products and l % 2 == 0:
                        prod[h, l, pl.ds(q, step), :] = b * sa[h, l, pl.ds(q, step), :] - a * sb[h, l, pl.ds(q, step), :]
                    elif products:
                        prod[h, l, pl.ds(q, step), :] = (
                            new_b * sb[h, l - 1, pl.ds(q, step), :] - new_a * sa[h, l - 1, pl.ds(q + 1, step), :])
            sweep(low, high, step, body)

    def collapse(q, n, more):
        start = q // LANES * LANES
        wanted = (lax.broadcasted_iota(jnp.int32, (n, LANES), 0) + (q - start)
                  == lax.broadcasted_iota(jnp.int32, (n, LANES), 1))
        for l in range(LAYERS):
            x = prod[0, l, q:q + n, :]
            for h in range(1, halves):
                x = x + prod[h, l, q:q + n, :]
            s = jnp.sum(x, axis=1, keepdims=True)
            line = jnp.sum(jnp.where(wanted, s, 0.0), axis=0, keepdims=True)
            if more:
                line = line + window[l:l + 1, start:start + LANES]
            window[l:l + 1, start:start + LANES] = line

    for pair in far_copies[1:]:
        for copy in pair:
            copy.start()

    for load in loads:
        load.wait()
    for copy in near_copies:
        copy.wait()
    edge = REACH + rows
    for h in range(halves):
        forward([h], q_own - 8, q_end + 8, 104, lambda h: field.at[h], 0, False)

        def emit(r, h=h):
            out[pl.ds(r, 128), h * LANES:(h + 1) * LANES] = field[h, pl.ds(r + REACH - first, 128), :]

        sweep(0, rows, 128, emit)
        field[h, REACH - 16:REACH, :] = zeros(16)
        field[h, edge:edge + 24, :] = zeros(24)
        cut[0:HALF, :] = field[h, rows:rows + HALF, :]
        whole = field.at[h]
        band(h, -HALF, 0, upper=whole)
        band(h, 0, rows, upper=whole, lower=whole)
        band(h, rows, rows + HALF, lower=cut, shift=rows)
        backward([h], q_lo, q_own + 8, 144, False)
        backward([h], q_own + 248, q_end - 248, 176, True)
        backward([h], q_end - 136, q_hi, 136, True)
    collapse(q_own + 264, 120, False)
    for q in range(q_own + 384, q_end - 384, LANES):
        collapse(q, LANES, False)
    collapse(q_end - 384, 120, False)
    collapse(q_end - 120, 120, False)

    for h in range(halves):
        for copy in far_copies[h]:
            copy.wait()
        raw[h, 8:8 + HALF, :] = far[h, 0]
        raw[h, FRONT + rows + 8:FRONT + rows + SENT, :] = far[h, 1]
        forward([h], q_lo, q_own, 136, lambda h: left_f, 0, True)
        forward([h], q_end - 8, q_hi, 144, lambda h: right_f, rows, True)
        left_f[2 * q_lo:HALF, :] = zeros(HALF - 2 * q_lo)
        left_f[REACH:REACH + 8, :] = zeros(8)
        right_f[REACH - 16:REACH, :] = zeros(16)
        right_f[REACH + HALF:REACH + HALF + 24, :] = zeros(24)
        band(h, 0, REACH, lower=left_f, more=True)
        band(h, rows - REACH, rows - HALF, upper=right_f, shift=rows, more=True)
        backward([h], q_own - 8, q_own + 264, 136, True)
        backward([h], q_end - 264, q_end - 120, 144, True)
    collapse(q_lo, 8, False)
    collapse(LANES, LANES, False)
    collapse(q_own, LANES, False)
    collapse(q_own + LANES, LANES, False)
    collapse(q_own + HALF, 8, True)
    collapse(q_end - 264, 8, True)
    collapse(q_end - HALF, LANES, False)
    collapse(q_end - LANES, 8, True)
    collapse(q_end, LANES, False)
    collapse(q_end + LANES, 8, False)

    whole = window[...]
    rolled = pltpu.roll(whole, 1, 1)
    odd = lax.broadcasted_iota(jnp.int32, whole.shape, 0) % 2 == 1
    moved = jnp.full(whole.shape, first, jnp.int32) == 1
    whole = jnp.where(jnp.logical_and(odd, moved), rolled, whole)[:LAYERS]
    mid = q_own + pairs // 2
    own_g[pl.ds(col, 1)] = jnp.concatenate([whole[:, q_own:mid], whole[:, mid:q_end]], 0)[None]
    send_l[...] = jnp.concatenate([whole[:, 0:LANES], whole[:, LANES:HALF]], 0)
    send_r[...] = jnp.concatenate([whole[:, q_end:q_end + LANES], whole[:, q_end + LANES:]], 0)
    copies = []
    for i, c in enumerate(others):
        copies.append(remote(own_g.at[col], own_g.at[col], o_send.at[i], o_recv.at[col], (blk, c)))
    for i, c in enumerate(every):
        copies.append(remote(send_l, right_g.at[col], l_send.at[i], l_recv.at[col], (before, c)))
        copies.append(remote(send_r, left_g.at[col], r_send.at[i], r_recv.at[col], (after, c)))
    for copy in copies:
        copy.start()
    for copy in copies:
        copy.wait_send()
    for i, c in enumerate(others):
        remote(own_g.at[c], own_g.at[c], o_send.at[i], o_recv.at[c], (blk, c)).wait_recv()
    for i, c in enumerate(every):
        remote(send_l, right_g.at[c], l_send.at[i], l_recv.at[c], (before, c)).wait_recv()
        remote(send_r, left_g.at[c], r_send.at[i], r_recv.at[c], (after, c)).wait_recv()
    own = own_g[0]
    left = left_g[0]
    right = right_g[0]
    for c in range(1, ncol):
        own = own + own_g[c]
        left = left + left_g[c]
        right = right + right_g[c]
    line = jnp.concatenate([own[:LAYERS], own[LAYERS:]], 1)
    line = jnp.concatenate([
        line[:, :LANES] + left[:LAYERS],
        line[:, LANES:HALF] + left[LAYERS:],
        line[:, HALF:pairs - HALF],
        line[:, pairs - HALF:pairs - LANES] + right[:LAYERS],
        line[:, pairs - LANES:] + right[LAYERS:],
    ], 1)
    grad[...] = line


def on_device(nblk, ncol, slab, angles, pairing, band_offsets, band_weights):
    rows, width = slab.shape
    halves = width // LANES
    pairs = rows // 2
    total_q = pairs + REACH
    buf_q = total_q + 8
    f32 = jnp.float32
    dma = pltpu.SemaphoreType.DMA
    smem = pl.BlockSpec(memory_space=pltpu.SMEM)
    anywhere = pl.BlockSpec(memory_space=pl.ANY)
    return pl.pallas_call(
        functools.partial(kernel, nblk, ncol),
        out_shape=(
            pltpu.VMEM((rows, width), f32),
            pltpu.VMEM((LAYERS, pairs), f32),
        ),
        in_specs=[smem, smem, smem, anywhere, anywhere],
        out_specs=(pl.BlockSpec(memory_space=pltpu.VMEM), pl.BlockSpec(memory_space=pltpu.VMEM)),
        scratch_shapes=[
            pltpu.VMEM((halves, FRONT + rows + SENT + 16, LANES), f32),
            pltpu.VMEM((halves, 2, HALF, LANES), f32),
            pltpu.VMEM((LAYERS, total_q), f32),
            pltpu.VMEM((2 * LAYERS, total_q, LANES), f32),
            pltpu.VMEM((halves, LAYERS - 1, buf_q, LANES), f32),
            pltpu.VMEM((halves, LAYERS - 1, buf_q, LANES), f32),
            pltpu.VMEM((halves, rows + 2 * REACH + 16, LANES), f32),
            pltpu.VMEM((2 * REACH + 8, LANES), f32),
            pltpu.VMEM((REACH + HALF + 24, LANES), f32),
            pltpu.VMEM((REACH + HALF, LANES), f32),
            pltpu.VMEM((halves, rows + 2 * REACH + 16, LANES), f32),
            pltpu.VMEM((halves, LAYERS - 1, buf_q, LANES), f32),
            pltpu.VMEM((halves, LAYERS - 1, buf_q, LANES), f32),
            pltpu.VMEM((halves, LAYERS, total_q, LANES), f32),
            pltpu.VMEM((2 * LAYERS, total_q), f32),
            pltpu.VMEM((ncol, 2 * LAYERS, pairs // 2), f32),
            pltpu.VMEM((ncol, 2 * LAYERS, LANES), f32),
            pltpu.VMEM((ncol, 2 * LAYERS, LANES), f32),
            pltpu.VMEM((2 * LAYERS, LANES), f32),
            pltpu.VMEM((2 * LAYERS, LANES), f32),
            dma((halves,)), dma,
            dma((halves, 2)), dma((halves, 2)),
            dma((halves, 2)), dma((halves, 2)),
            dma((2,)), dma((2,)),
            dma((ncol - 1,)), dma((ncol,)),
            dma((ncol,)), dma((ncol,)),
            dma((ncol,)), dma((ncol,)),
        ],
        compiler_params=pltpu.CompilerParams(
            collective_id=0, has_side_effects=True, vmem_limit_bytes=58 * 2**20),
    )(pairing, band_offsets, band_weights, slab, angles)


def solution(mesh):
    in_specs = (P("blk", "col"), P(None, "blk"), P(), P(), P())
    out_specs = (P("blk", "col"), P(None, "blk"))
    return jax.shard_map(
        functools.partial(on_device, mesh.shape["blk"], mesh.shape["col"]),
        mesh=mesh, in_specs=in_specs, out_specs=out_specs, check_vma=False,
    )
```

```python
import functools

import jax
import jax.numpy as jnp
from jax import lax
from jax.experimental import pallas as pl
from jax.experimental.pallas import tpu as pltpu
from jax.sharding import PartitionSpec as P

LAYERS = 4
BANDS = 8
REACH = 512
HALF = REACH // 2
SENT = HALF + 8
LANES = 128
FRONT = SENT + 8
MESH = pl.DeviceIdType.MESH


def sweep(low, high, step, body):
    assert (high - low) % step == 0 and low % 8 == 0 and step % 8 == 0
    if high - low == step:
        body(low)
        return

    def one(i, carry):
        body(pl.multiple_of(low + i * step, 8))
        return carry

    lax.fori_loop(0, (high - low) // step, one, 0)


def sin_cos(x):
    n = jnp.floor(x * 0.6366197723675814 + 0.5)
    r = ((x - n * 1.5703125) - n * 4.837512969970703e-4) - n * 7.54978995489188e-8
    z = r * r
    s = ((-1.9515295891e-4 * z + 8.3321608736e-3) * z - 1.6666654611e-1) * z * r + r
    c = ((2.443315711809948e-5 * z - 1.388731625493765e-3) * z + 4.166664568298827e-2) * z * z - 0.5 * z + 1.0
    odd = jnp.abs(n) == 1.0
    even_sign = jnp.where(n == 0.0, 1.0, -1.0)
    return jnp.where(odd, n * c, even_sign * s), jnp.where(odd, -n * s, even_sign * c)


def kernel(
    nblk, ncol,
    pairing, offsets, weights, slab, angles,
    out, grad,
    raw, near, far, angw, coef, sa, sb, field, left_f, right_f, cut, adj, xa, xb, prod, window,
    own_g, left_g, right_g, send_l, send_r,
    load_sem, ang_sem, n_send, n_recv, h_send, h_recv, a_send, a_recv,
    o_send, o_recv, l_send, l_recv, r_send, r_recv,
):
    rows, width = slab.shape
    halves = width // LANES
    pairs = rows // 2
    q_own = HALF
    q_end = q_own + pairs
    q_lo, q_hi = 120, q_end + 136
    total_q = pairs + REACH
    blk = lax.axis_index("blk")
    col = lax.axis_index("col")
    after = lax.rem(blk + 1, nblk)
    before = lax.rem(blk + nblk - 1, nblk)
    others = [lax.rem(col + d, ncol) for d in range(1, ncol)]
    every = [col] + others

    barrier = pltpu.get_barrier_semaphore()
    peers = [(blk, c) for c in others] + [(b, c) for b in (after, before) for c in every]
    for peer in peers:
        pl.semaphore_signal(barrier, inc=1, device_id=peer, device_id_type=MESH)

    loads = []
    for h in range(halves):
        loads.append(pltpu.make_async_copy(
            slab.at[:, pl.ds(h * LANES, LANES)], raw.at[h, pl.ds(FRONT, rows)], load_sem.at[h]))
    own_ang = pltpu.make_async_copy(angles, angw.at[:, pl.ds(HALF, pairs)], ang_sem)
    own_ang.start()
    for load in loads:
        load.start()

    def remote(src, dst, s, r, peer):
        return pltpu.make_async_remote_copy(
            src_ref=src, dst_ref=dst, send_sem=s, recv_sem=r, device_id=peer, device_id_type=MESH)

    ang_copies = [
        remote(angles.at[:, pl.ds(pairs - HALF, HALF)], angw.at[:, pl.ds(0, HALF)], a_send.at[0], a_recv.at[0], (after, col)),
        remote(angles.at[:, pl.ds(0, HALF)], angw.at[:, pl.ds(q_end, HALF)], a_send.at[1], a_recv.at[1], (before, col)),
    ]
    near_copies = []
    far_copies = []
    for h in range(halves):
        lanes = pl.ds(h * LANES, LANES)
        near_copies += [
            remote(slab.at[pl.ds(rows - 8, 8), lanes], near.at[h, 0], n_send.at[h, 0], n_recv.at[h, 0], (after, col)),
            remote(slab.at[pl.ds(0, 8), lanes], near.at[h, 1], n_send.at[h, 1], n_recv.at[h, 1], (before, col)),
        ]
        far_copies.append([
            remote(slab.at[pl.ds(rows - SENT, HALF), lanes], far.at[h, 0], h_send.at[h, 0], h_recv.at[h, 0], (after, col)),
            remote(slab.at[pl.ds(8, HALF), lanes], far.at[h, 1], h_send.at[h, 1], h_recv.at[h, 1], (before, col)),
        ])

    first = pairing[0]

    def zeros(n):
        return jnp.zeros((n, LANES), jnp.float32)

    left_f[...] = zeros(left_f.shape[0])
    right_f[...] = zeros(right_f.shape[0])
    cut[...] = zeros(cut.shape[0])
    for h in range(halves):
        raw[h, 0:8, :] = zeros(8)
        raw[h, FRONT + rows + SENT:FRONT + rows + SENT + 16, :] = zeros(16)
        adj[h, 2 * q_lo:REACH - HALF, :] = zeros(REACH - HALF - 2 * q_lo)
        top = REACH + rows + HALF
        adj[h, top:2 * q_hi + 8, :] = zeros(2 * q_hi + 8 - top)
        field[h, 0:REACH, :] = zeros(REACH)
        field[h, REACH + rows:, :] = zeros(field.shape[1] - REACH - rows)
        for l in range(LAYERS - 1):
            sa[h, l, q_hi:q_hi + 8, :] = zeros(8)
            sb[h, l, q_lo - 8:q_lo, :] = zeros(8)
            xb[h, l, q_lo - 8:q_lo, :] = zeros(8)
            xa[h, l, q_hi:q_hi + 8, :] = zeros(8)

    def coefficients(theta):
        mid = theta.shape[1] // 2
        sine, cosine = sin_cos(jnp.concatenate([theta[:, :mid], theta[:, mid:]], 0))
        return jnp.concatenate([
            jnp.concatenate([cosine[:LAYERS], sine[:LAYERS]], 0),
            jnp.concatenate([cosine[LAYERS:], sine[LAYERS:]], 0)], 1)

    def aligned(both):
        rolled = pltpu.roll(both, both.shape[1] - 1, 1)
        odd = lax.broadcasted_iota(jnp.int32, both.shape, 0) % 2 == 1
        moved = jnp.full(both.shape, first, jnp.int32) == 1
        return jnp.where(jnp.logical_and(odd, moved), rolled, both)

    def spread(q, low=0, n=LANES):
        turned = window[:, q:q + LANES].T[low:low + n]
        for j in range(2 * LAYERS):
            coef[j, q + low:q + low + n, :] = jnp.broadcast_to(turned[:, j:j + 1], (n, LANES))

    own_ang.wait()
    own_both = coefficients(angw[:, q_own:q_end])
    window[:, q_own:q_end] = aligned(own_both)
    for q in range(q_own, q_end - LANES, LANES):
        spread(q)

    pl.semaphore_wait(barrier, len(peers))
    for copy in ang_copies + near_copies + far_copies[0]:
        copy.start()

    def held(h, l, q, n):
        if l == LAYERS - 1:
            return adj[h, pl.ds(2 * q + 1, n, stride=2), :], adj[h, pl.ds(2 * q + 2, n, stride=2), :]
        if l % 2 == 1:
            return xb[h, l, pl.ds(q, n), :], xa[h, l, pl.ds(q + 1, n), :]
        return xb[h, l, pl.ds(q - 1, n), :], xa[h, l, pl.ds(q, n), :]

    def forward(halves_in, low, high, step, target, shift, products):
        for l in range(LAYERS):
            def body(q, l=l):
                c = coef[l, pl.ds(q, step), :]
                s = coef[LAYERS + l, pl.ds(q, step), :]
                for h in halves_in:
                    if l == 0:
                        a = raw[h, pl.ds(2 * q - 2 * q_lo + first, step, stride=2), :]
                        b = raw[h, pl.ds(2 * q - 2 * q_lo + 1 + first, step, stride=2), :]
                    elif l % 2 == 1:
                        a = sb[h, l - 1, pl.ds(q, step), :]
                        b = sa[h, l - 1, pl.ds(q + 1, step), :]
                    else:
                        a = sb[h, l - 1, pl.ds(q - 1, step), :]
                        b = sa[h, l - 1, pl.ds(q, step), :]
                    new_a = c * a - s * b
                    new_b = s * a + c * b
                    if l < LAYERS - 1:
                        sa[h, l, pl.ds(q, step), :] = new_a
                        sb[h, l, pl.ds(q, step), :] = new_b
                    if products:
                        a, b = held(h, l, q, step)
                        prod[h, l, pl.ds(q, step), :] = b * new_a - a * new_b
                    if l == LAYERS - 1:
                        into = target(h)
                        into[pl.ds(2 * q + 1 - shift, step, stride=2), :] = new_a
                        into[pl.ds(2 * q + 2 - shift, step, stride=2), :] = new_b
            sweep(low, high, step, body)

    reach = [offsets[k] for k in range(BANDS)]
    weight = [weights[k] for k in range(BANDS)]

    def band(h, low, high, upper=None, lower=None, shift=0, more=False):
        n = 128

        def body(t):
            acc = adj[h, pl.ds(t, n), :] if more else None
            for k in range(BANDS):
                part = None
                if upper is not None:
                    part = upper[pl.ds(t - shift + reach[k], n), :]
                if lower is not None:
                    down = lower[pl.ds(t - shift - reach[k], n), :]
                    part = down if part is None else part + down
                part = weight[k] * part
                acc = part if acc is None else acc + part
            adj[h, pl.ds(t, n), :] = acc
        sweep(low + REACH, high + REACH, n, body)

    def backward(halves_in, low, high, step, products):
        for l in reversed(range(LAYERS)):
            if l == 0 and not products:
                continue

            def body(q, l=l):
                if l > 0:
                    c = coef[l, pl.ds(q, step), :]
                    s = coef[LAYERS + l, pl.ds(q, step), :]
                for h in halves_in:
                    a, b = held(h, l, q, step)
                    if l > 0:
                        new_a = c * a + s * b
                        new_b = c * b - s * a
                        xa[h, l - 1, pl.ds(q, step), :] = new_a
                        xb[h, l - 1, pl.ds(q, step), :] = new_b
                    if products and l % 2 == 0:
                        prod[h, l, pl.ds(q, step), :] = b * sa[h, l, pl.ds(q, step), :] - a * sb[h, l, pl.ds(q, step), :]
                    elif products:
                        prod[h, l, pl.ds(q, step), :] = (
                            new_b * sb[h, l - 1, pl.ds(q, step), :] - new_a * sa[h, l - 1, pl.ds(q + 1, step), :])
            sweep(low, high, step, body)

    def collapse(q, n, more):
        start = q // LANES * LANES
        wanted = (lax.broadcasted_iota(jnp.int32, (n, LANES), 0) + (q - start)
                  == lax.broadcasted_iota(jnp.int32, (n, LANES), 1))
        for l in range(LAYERS):
            x = prod[0, l, q:q + n, :]
            for h in range(1, halves):
                x = x + prod[h, l, q:q + n, :]
            s = jnp.sum(x, axis=1, keepdims=True)
            line = jnp.sum(jnp.where(wanted, s, 0.0), axis=0, keepdims=True)
            if more:
                line = line + window[l:l + 1, start:start + LANES]
            window[l:l + 1, start:start + LANES] = line

    for load in loads:
        load.wait()
    for h in range(halves):
        forward([h], q_own, q_end - LANES, 112, lambda h: field.at[h], 0, False)
        if h == 0:
            for pair in far_copies[1:]:
                for copy in pair:
                    copy.start()

    for copy in ang_copies:
        copy.wait()
    left_both = coefficients(angw[:, :q_own])
    right_both = coefficients(angw[:, q_end:])
    window[...] = aligned(jnp.concatenate([left_both, own_both, right_both], 1))
    spread(0, q_lo, 8)
    for q in (LANES, q_end - LANES, q_end):
        spread(q)
    spread(q_end + LANES, 0, 8)
    for copy in near_copies:
        copy.wait()
    for h in range(halves):
        raw[h, FRONT - 8:FRONT, :] = near[h, 0]
        raw[h, FRONT + rows:FRONT + rows + 8, :] = near[h, 1]
    edge = REACH + rows
    for h in range(halves):
        forward([h], q_own - 8, q_own + 8, 16, lambda h: field.at[h], 0, False)
        forward([h], q_end - 136, q_end + 8, 144, lambda h: field.at[h], 0, False)

        def emit(r, h=h):
            out[pl.ds(r, 128), h * LANES:(h + 1) * LANES] = field[h, pl.ds(r + REACH - first, 128), :]

        sweep(0, rows, 128, emit)
        field[h, REACH - 16:REACH, :] = zeros(16)
        field[h, edge:edge + 24, :] = zeros(24)
        cut[0:HALF, :] = field[h, rows:rows + HALF, :]
        whole = field.at[h]
        band(h, -HALF, 0, upper=whole)
        band(h, 0, rows, upper=whole, lower=whole)
        band(h, rows, rows + HALF, lower=cut, shift=rows)
        backward([h], q_lo, q_own + 8, 144, False)
        backward([h], q_own + 248, q_end - 248, 176, True)
        backward([h], q_end - 136, q_hi, 136, True)
    collapse(q_own + 264, 120, False)
    for q in range(q_own + 384, q_end - 384, LANES):
        collapse(q, LANES, False)
    collapse(q_end - 384, 120, False)
    collapse(q_end - 120, 120, False)

    for h in range(halves):
        for copy in far_copies[h]:
            copy.wait()
        raw[h, 8:8 + HALF, :] = far[h, 0]
        raw[h, FRONT + rows + 8:FRONT + rows + SENT, :] = far[h, 1]
        forward([h], q_lo, q_own, 136, lambda h: left_f, 0, True)
        forward([h], q_end - 8, q_hi, 144, lambda h: right_f, rows, True)
        left_f[2 * q_lo:HALF, :] = zeros(HALF - 2 * q_lo)
        left_f[REACH:REACH + 8, :] = zeros(8)
        right_f[REACH - 16:REACH, :] = zeros(16)
        right_f[REACH + HALF:REACH + HALF + 24, :] = zeros(24)
        band(h, 0, REACH, lower=left_f, more=True)
        band(h, rows - REACH, rows - HALF, upper=right_f, shift=rows, more=True)
        backward([h], q_own - 8, q_own + 264, 136, True)
        backward([h], q_end - 264, q_end - 120, 144, True)
    collapse(q_lo, 8, False)
    collapse(LANES, LANES, False)
    collapse(q_own, LANES, False)
    collapse(q_own + LANES, LANES, False)
    collapse(q_own + HALF, 8, True)
    collapse(q_end - 264, 8, True)
    collapse(q_end - HALF, LANES, False)
    collapse(q_end - LANES, 8, True)
    collapse(q_end, LANES, False)
    collapse(q_end + LANES, 8, False)

    whole = window[...]
    rolled = pltpu.roll(whole, 1, 1)
    odd = lax.broadcasted_iota(jnp.int32, whole.shape, 0) % 2 == 1
    moved = jnp.full(whole.shape, first, jnp.int32) == 1
    whole = jnp.where(jnp.logical_and(odd, moved), rolled, whole)[:LAYERS]
    mid = q_own + pairs // 2
    own_g[pl.ds(col, 1)] = jnp.concatenate([whole[:, q_own:mid], whole[:, mid:q_end]], 0)[None]
    send_l[...] = jnp.concatenate([whole[:, 0:LANES], whole[:, LANES:HALF]], 0)
    send_r[...] = jnp.concatenate([whole[:, q_end:q_end + LANES], whole[:, q_end + LANES:]], 0)
    copies = []
    for i, c in enumerate(others):
        copies.append(remote(own_g.at[col], own_g.at[col], o_send.at[i], o_recv.at[col], (blk, c)))
    for i, c in enumerate(every):
        copies.append(remote(send_l, right_g.at[col], l_send.at[i], l_recv.at[col], (before, c)))
        copies.append(remote(send_r, left_g.at[col], r_send.at[i], r_recv.at[col], (after, c)))
    for copy in copies:
        copy.start()
    for copy in copies:
        copy.wait_send()
    for i, c in enumerate(others):
        remote(own_g.at[c], own_g.at[c], o_send.at[i], o_recv.at[c], (blk, c)).wait_recv()
    for i, c in enumerate(every):
        remote(send_l, right_g.at[c], l_send.at[i], l_recv.at[c], (before, c)).wait_recv()
        remote(send_r, left_g.at[c], r_send.at[i], r_recv.at[c], (after, c)).wait_recv()
    own = own_g[0]
    left = left_g[0]
    right = right_g[0]
    for c in range(1, ncol):
        own = own + own_g[c]
        left = left + left_g[c]
        right = right + right_g[c]
    line = jnp.concatenate([own[:LAYERS], own[LAYERS:]], 1)
    line = jnp.concatenate([
        line[:, :LANES] + left[:LAYERS],
        line[:, LANES:HALF] + left[LAYERS:],
        line[:, HALF:pairs - HALF],
        line[:, pairs - HALF:pairs - LANES] + right[:LAYERS],
        line[:, pairs - LANES:] + right[LAYERS:],
    ], 1)
    grad[...] = line


def on_device(nblk, ncol, slab, angles, pairing, band_offsets, band_weights):
    rows, width = slab.shape
    halves = width // LANES
    pairs = rows // 2
    total_q = pairs + REACH
    buf_q = total_q + 8
    f32 = jnp.float32
    dma = pltpu.SemaphoreType.DMA
    smem = pl.BlockSpec(memory_space=pltpu.SMEM)
    anywhere = pl.BlockSpec(memory_space=pl.ANY)
    return pl.pallas_call(
        functools.partial(kernel, nblk, ncol),
        out_shape=(
            pltpu.VMEM((rows, width), f32),
            pltpu.VMEM((LAYERS, pairs), f32),
        ),
        in_specs=[smem, smem, smem, anywhere, anywhere],
        out_specs=(pl.BlockSpec(memory_space=pltpu.VMEM), pl.BlockSpec(memory_space=pltpu.VMEM)),
        scratch_shapes=[
            pltpu.VMEM((halves, FRONT + rows + SENT + 16, LANES), f32),
            pltpu.VMEM((halves, 2, 8, LANES), f32),
            pltpu.VMEM((halves, 2, HALF, LANES), f32),
            pltpu.VMEM((LAYERS, total_q), f32),
            pltpu.VMEM((2 * LAYERS, total_q, LANES), f32),
            pltpu.VMEM((halves, LAYERS - 1, buf_q, LANES), f32),
            pltpu.VMEM((halves, LAYERS - 1, buf_q, LANES), f32),
            pltpu.VMEM((halves, rows + 2 * REACH + 16, LANES), f32),
            pltpu.VMEM((2 * REACH + 8, LANES), f32),
            pltpu.VMEM((REACH + HALF + 24, LANES), f32),
            pltpu.VMEM((REACH + HALF, LANES), f32),
            pltpu.VMEM((halves, rows + 2 * REACH + 16, LANES), f32),
            pltpu.VMEM((halves, LAYERS - 1, buf_q, LANES), f32),
            pltpu.VMEM((halves, LAYERS - 1, buf_q, LANES), f32),
            pltpu.VMEM((halves, LAYERS, total_q, LANES), f32),
            pltpu.VMEM((2 * LAYERS, total_q), f32),
            pltpu.VMEM((ncol, 2 * LAYERS, pairs // 2), f32),
            pltpu.VMEM((ncol, 2 * LAYERS, LANES), f32),
            pltpu.VMEM((ncol, 2 * LAYERS, LANES), f32),
            pltpu.VMEM((2 * LAYERS, LANES), f32),
            pltpu.VMEM((2 * LAYERS, LANES), f32),
            dma((halves,)), dma,
            dma((halves, 2)), dma((halves, 2)),
            dma((halves, 2)), dma((halves, 2)),
            dma((2,)), dma((2,)),
            dma((ncol - 1,)), dma((ncol,)),
            dma((ncol,)), dma((ncol,)),
            dma((ncol,)), dma((ncol,)),
        ],
        compiler_params=pltpu.CompilerParams(
            collective_id=0, has_side_effects=True, vmem_limit_bytes=58 * 2**20),
    )(pairing, band_offsets, band_weights, slab, angles)


def solution(mesh):
    in_specs = (P("blk", "col"), P(None, "blk"), P(), P(), P())
    out_specs = (P("blk", "col"), P(None, "blk"))
    return jax.shard_map(
        functools.partial(on_device, mesh.shape["blk"], mesh.shape["col"]),
        mesh=mesh, in_specs=in_specs, out_specs=out_specs, check_vma=False,
    )
```

```python
import functools

import jax
import jax.numpy as jnp
from jax import lax
from jax.experimental import pallas as pl
from jax.experimental.pallas import tpu as pltpu
from jax.sharding import PartitionSpec as P

LAYERS = 4
BANDS = 8
REACH = 512
HALF = REACH // 2
SENT = HALF + 8
LANES = 128
FRONT = SENT + 8
MESH = pl.DeviceIdType.MESH


def sweep(low, high, step, body):
    assert (high - low) % step == 0 and low % 8 == 0 and step % 8 == 0
    if high - low == step:
        body(low)
        return

    def one(i, carry):
        body(pl.multiple_of(low + i * step, 8))
        return carry

    lax.fori_loop(0, (high - low) // step, one, 0)


def sin_cos(x):
    n = jnp.floor(x * 0.6366197723675814 + 0.5)
    r = ((x - n * 1.5703125) - n * 4.837512969970703e-4) - n * 7.54978995489188e-8
    z = r * r
    s = ((-1.9515295891e-4 * z + 8.3321608736e-3) * z - 1.6666654611e-1) * z * r + r
    c = ((2.443315711809948e-5 * z - 1.388731625493765e-3) * z + 4.166664568298827e-2) * z * z - 0.5 * z + 1.0
    odd = jnp.abs(n) == 1.0
    even_sign = jnp.where(n == 0.0, 1.0, -1.0)
    return jnp.where(odd, n * c, even_sign * s), jnp.where(odd, -n * s, even_sign * c)


def kernel(
    nblk, ncol,
    pairing, offsets, weights, slab, angles,
    out, grad,
    raw, near, far, angw, coef, sa, sb, field, left_f, right_f, cut, adj, xa, xb, prod, window,
    own_g, left_g, right_g, send_l, send_r,
    load_sem, ang_sem, n_send, n_recv, h_send, h_recv, a_send, a_recv,
    o_send, o_recv, l_send, l_recv, r_send, r_recv,
):
    rows, width = slab.shape
    halves = width // LANES
    pairs = rows // 2
    q_own = HALF
    q_end = q_own + pairs
    q_lo, q_hi = 120, q_end + 136
    total_q = pairs + REACH
    blk = lax.axis_index("blk")
    col = lax.axis_index("col")
    after = lax.rem(blk + 1, nblk)
    before = lax.rem(blk + nblk - 1, nblk)
    others = [lax.rem(col + d, ncol) for d in range(1, ncol)]
    every = [col] + others

    barrier = pltpu.get_barrier_semaphore()
    peers = [(blk, c) for c in others] + [(b, c) for b in (after, before) for c in every]
    for peer in peers:
        pl.semaphore_signal(barrier, inc=1, device_id=peer, device_id_type=MESH)

    loads = []
    for h in range(halves):
        loads.append(pltpu.make_async_copy(
            slab.at[:, pl.ds(h * LANES, LANES)], raw.at[h, pl.ds(FRONT, rows)], load_sem.at[h]))
    own_ang = pltpu.make_async_copy(angles, angw.at[:, pl.ds(HALF, pairs)], ang_sem)
    own_ang.start()
    for load in loads:
        load.start()

    def remote(src, dst, s, r, peer):
        return pltpu.make_async_remote_copy(
            src_ref=src, dst_ref=dst, send_sem=s, recv_sem=r, device_id=peer, device_id_type=MESH)

    ang_copies = [
        remote(angles.at[:, pl.ds(pairs - HALF, HALF)], angw.at[:, pl.ds(0, HALF)], a_send.at[0], a_recv.at[0], (after, col)),
        remote(angles.at[:, pl.ds(0, HALF)], angw.at[:, pl.ds(q_end, HALF)], a_send.at[1], a_recv.at[1], (before, col)),
    ]
    near_copies = []
    far_copies = []
    for h in range(halves):
        lanes = pl.ds(h * LANES, LANES)
        near_copies += [
            remote(slab.at[pl.ds(rows - 8, 8), lanes], near.at[h, 0], n_send.at[h, 0], n_recv.at[h, 0], (after, col)),
            remote(slab.at[pl.ds(0, 8), lanes], near.at[h, 1], n_send.at[h, 1], n_recv.at[h, 1], (before, col)),
        ]
        far_copies.append([
            remote(slab.at[pl.ds(rows - SENT, HALF), lanes], far.at[h, 0], h_send.at[h, 0], h_recv.at[h, 0], (after, col)),
            remote(slab.at[pl.ds(8, HALF), lanes], far.at[h, 1], h_send.at[h, 1], h_recv.at[h, 1], (before, col)),
        ])

    first = pairing[0]

    pl.semaphore_wait(barrier, len(peers))
    for copy in ang_copies + near_copies + far_copies[0]:
        copy.start()

    def zeros(n):
        return jnp.zeros((n, LANES), jnp.float32)

    left_f[...] = zeros(left_f.shape[0])
    right_f[...] = zeros(right_f.shape[0])
    cut[...] = zeros(cut.shape[0])
    for h in range(halves):
        raw[h, 0:8, :] = zeros(8)
        raw[h, FRONT + rows + SENT:FRONT + rows + SENT + 16, :] = zeros(16)
        adj[h, 2 * q_lo:REACH - HALF, :] = zeros(REACH - HALF - 2 * q_lo)
        top = REACH + rows + HALF
        adj[h, top:2 * q_hi + 8, :] = zeros(2 * q_hi + 8 - top)
        field[h, 0:REACH, :] = zeros(REACH)
        field[h, REACH + rows:, :] = zeros(field.shape[1] - REACH - rows)
        for l in range(LAYERS - 1):
            sa[h, l, q_hi:q_hi + 8, :] = zeros(8)
            sb[h, l, q_lo - 8:q_lo, :] = zeros(8)
            xb[h, l, q_lo - 8:q_lo, :] = zeros(8)
            xa[h, l, q_hi:q_hi + 8, :] = zeros(8)

    def coefficients(theta):
        mid = theta.shape[1] // 2
        sine, cosine = sin_cos(jnp.concatenate([theta[:, :mid], theta[:, mid:]], 0))
        return jnp.concatenate([
            jnp.concatenate([cosine[:LAYERS], sine[:LAYERS]], 0),
            jnp.concatenate([cosine[LAYERS:], sine[LAYERS:]], 0)], 1)

    def aligned(both):
        rolled = pltpu.roll(both, both.shape[1] - 1, 1)
        odd = lax.broadcasted_iota(jnp.int32, both.shape, 0) % 2 == 1
        moved = jnp.full(both.shape, first, jnp.int32) == 1
        return jnp.where(jnp.logical_and(odd, moved), rolled, both)

    def spread(q, low=0, n=LANES):
        turned = window[:, q:q + LANES].T[low:low + n]
        for j in range(2 * LAYERS):
            coef[j, q + low:q + low + n, :] = jnp.broadcast_to(turned[:, j:j + 1], (n, LANES))

    own_ang.wait()
    own_both = coefficients(angw[:, q_own:q_end])
    window[:, q_own:q_end] = aligned(own_both)
    for q in range(q_own, q_end - LANES, LANES):
        spread(q)

    def held(h, l, q, n):
        if l == LAYERS - 1:
            return adj[h, pl.ds(2 * q + 1, n, stride=2), :], adj[h, pl.ds(2 * q + 2, n, stride=2), :]
        if l % 2 == 1:
            return xb[h, l, pl.ds(q, n), :], xa[h, l, pl.ds(q + 1, n), :]
        return xb[h, l, pl.ds(q - 1, n), :], xa[h, l, pl.ds(q, n), :]

    def forward(halves_in, low, high, step, target, shift, products):
        for l in range(LAYERS):
            def body(q, l=l):
                c = coef[l, pl.ds(q, step), :]
                s = coef[LAYERS + l, pl.ds(q, step), :]
                for h in halves_in:
                    if l == 0:
                        a = raw[h, pl.ds(2 * q - 2 * q_lo + first, step, stride=2), :]
                        b = raw[h, pl.ds(2 * q - 2 * q_lo + 1 + first, step, stride=2), :]
                    elif l % 2 == 1:
                        a = sb[h, l - 1, pl.ds(q, step), :]
                        b = sa[h, l - 1, pl.ds(q + 1, step), :]
                    else:
                        a = sb[h, l - 1, pl.ds(q - 1, step), :]
                        b = sa[h, l - 1, pl.ds(q, step), :]
                    new_a = c * a - s * b
                    new_b = s * a + c * b
                    if l < LAYERS - 1:
                        sa[h, l, pl.ds(q, step), :] = new_a
                        sb[h, l, pl.ds(q, step), :] = new_b
                    if products:
                        a, b = held(h, l, q, step)
                        prod[h, l, pl.ds(q, step), :] = b * new_a - a * new_b
                    if l == LAYERS - 1:
                        into = target(h)
                        into[pl.ds(2 * q + 1 - shift, step, stride=2), :] = new_a
                        into[pl.ds(2 * q + 2 - shift, step, stride=2), :] = new_b
            sweep(low, high, step, body)

    reach = [offsets[k] for k in range(BANDS)]
    weight = [weights[k] for k in range(BANDS)]

    def band(h, low, high, upper=None, lower=None, shift=0, more=False):
        n = 128

        def body(t):
            acc = adj[h, pl.ds(t, n), :] if more else None
            for k in range(BANDS):
                part = None
                if upper is not None:
                    part = upper[pl.ds(t - shift + reach[k], n), :]
                if lower is not None:
                    down = lower[pl.ds(t - shift - reach[k], n), :]
                    part = down if part is None else part + down
                part = weight[k] * part
                acc = part if acc is None else acc + part
            adj[h, pl.ds(t, n), :] = acc
        sweep(low + REACH, high + REACH, n, body)

    def backward(halves_in, low, high, step, products):
        for l in reversed(range(LAYERS)):
            if l == 0 and not products:
                continue

            def body(q, l=l):
                if l > 0:
                    c = coef[l, pl.ds(q, step), :]
                    s = coef[LAYERS + l, pl.ds(q, step), :]
                for h in halves_in:
                    a, b = held(h, l, q, step)
                    if l > 0:
                        new_a = c * a + s * b
                        new_b = c * b - s * a
                        xa[h, l - 1, pl.ds(q, step), :] = new_a
                        xb[h, l - 1, pl.ds(q, step), :] = new_b
                    if products and l % 2 == 0:
                        prod[h, l, pl.ds(q, step), :] = b * sa[h, l, pl.ds(q, step), :] - a * sb[h, l, pl.ds(q, step), :]
                    elif products:
                        prod[h, l, pl.ds(q, step), :] = (
                            new_b * sb[h, l - 1, pl.ds(q, step), :] - new_a * sa[h, l - 1, pl.ds(q + 1, step), :])
            sweep(low, high, step, body)

    def collapse(q, n, more):
        start = q // LANES * LANES
        wanted = (lax.broadcasted_iota(jnp.int32, (n, LANES), 0) + (q - start)
                  == lax.broadcasted_iota(jnp.int32, (n, LANES), 1))
        for l in range(LAYERS):
            x = prod[0, l, q:q + n, :]
            for h in range(1, halves):
                x = x + prod[h, l, q:q + n, :]
            s = jnp.sum(x, axis=1, keepdims=True)
            line = jnp.sum(jnp.where(wanted, s, 0.0), axis=0, keepdims=True)
            if more:
                line = line + window[l:l + 1, start:start + LANES]
            window[l:l + 1, start:start + LANES] = line

    for load in loads:
        load.wait()
    for h in range(halves):
        forward([h], q_own, q_end - LANES, 112, lambda h: field.at[h], 0, False)
    for pair in far_copies[1:]:
        for copy in pair:
            copy.start()

    for copy in ang_copies:
        copy.wait()
    left_both = coefficients(angw[:, :q_own])
    right_both = coefficients(angw[:, q_end:])
    window[...] = aligned(jnp.concatenate([left_both, own_both, right_both], 1))
    spread(0, q_lo, 8)
    for q in (LANES, q_end - LANES, q_end):
        spread(q)
    spread(q_end + LANES, 0, 8)
    for copy in near_copies:
        copy.wait()
    for h in range(halves):
        raw[h, FRONT - 8:FRONT, :] = near[h, 0]
        raw[h, FRONT + rows:FRONT + rows + 8, :] = near[h, 1]
    edge = REACH + rows
    for h in range(halves):
        forward([h], q_own - 8, q_own + 8, 16, lambda h: field.at[h], 0, False)
        forward([h], q_end - 136, q_end + 8, 144, lambda h: field.at[h], 0, False)

        def emit(r, h=h):
            out[pl.ds(r, 128), h * LANES:(h + 1) * LANES] = field[h, pl.ds(r + REACH - first, 128), :]

        sweep(0, rows, 128, emit)
        field[h, REACH - 16:REACH, :] = zeros(16)
        field[h, edge:edge + 24, :] = zeros(24)
        cut[0:HALF, :] = field[h, rows:rows + HALF, :]
        whole = field.at[h]
        band(h, -HALF, 0, upper=whole)
        band(h, 0, rows, upper=whole, lower=whole)
        band(h, rows, rows + HALF, lower=cut, shift=rows)
        backward([h], q_lo, q_own + 8, 144, False)
        backward([h], q_own + 248, q_end - 248, 176, True)
        backward([h], q_end - 136, q_hi, 136, True)
    collapse(q_own + 264, 120, False)
    for q in range(q_own + 384, q_end - 384, LANES):
        collapse(q, LANES, False)
    collapse(q_end - 384, 120, False)
    collapse(q_end - 120, 120, False)

    for h in range(halves):
        for copy in far_copies[h]:
            copy.wait()
        raw[h, 8:8 + HALF, :] = far[h, 0]
        raw[h, FRONT + rows + 8:FRONT + rows + SENT, :] = far[h, 1]
        forward([h], q_lo, q_own, 136, lambda h: left_f, 0, True)
        forward([h], q_end - 8, q_hi, 144, lambda h: right_f, rows, True)
        left_f[2 * q_lo:HALF, :] = zeros(HALF - 2 * q_lo)
        left_f[REACH:REACH + 8, :] = zeros(8)
        right_f[REACH - 16:REACH, :] = zeros(16)
        right_f[REACH + HALF:REACH + HALF + 24, :] = zeros(24)
        band(h, 0, REACH, lower=left_f, more=True)
        band(h, rows - REACH, rows - HALF, upper=right_f, shift=rows, more=True)
        backward([h], q_own - 8, q_own + 264, 136, True)
        backward([h], q_end - 264, q_end - 120, 144, True)
    collapse(q_lo, 8, False)
    collapse(LANES, LANES, False)
    collapse(q_own, LANES, False)
    collapse(q_own + LANES, LANES, False)
    collapse(q_own + HALF, 8, True)
    collapse(q_end - 264, 8, True)
    collapse(q_end - HALF, LANES, False)
    collapse(q_end - LANES, 8, True)
    collapse(q_end, LANES, False)
    collapse(q_end + LANES, 8, False)

    whole = window[...]
    rolled = pltpu.roll(whole, 1, 1)
    odd = lax.broadcasted_iota(jnp.int32, whole.shape, 0) % 2 == 1
    moved = jnp.full(whole.shape, first, jnp.int32) == 1
    whole = jnp.where(jnp.logical_and(odd, moved), rolled, whole)[:LAYERS]
    mid = q_own + pairs // 2
    own_g[pl.ds(col, 1)] = jnp.concatenate([whole[:, q_own:mid], whole[:, mid:q_end]], 0)[None]
    send_l[...] = jnp.concatenate([whole[:, 0:LANES], whole[:, LANES:HALF]], 0)
    send_r[...] = jnp.concatenate([whole[:, q_end:q_end + LANES], whole[:, q_end + LANES:]], 0)
    copies = []
    for i, c in enumerate(others):
        copies.append(remote(own_g.at[col], own_g.at[col], o_send.at[i], o_recv.at[col], (blk, c)))
    for i, c in enumerate(every):
        copies.append(remote(send_l, right_g.at[col], l_send.at[i], l_recv.at[col], (before, c)))
        copies.append(remote(send_r, left_g.at[col], r_send.at[i], r_recv.at[col], (after, c)))
    for copy in copies:
        copy.start()
    for copy in copies:
        copy.wait_send()
    for i, c in enumerate(others):
        remote(own_g.at[c], own_g.at[c], o_send.at[i], o_recv.at[c], (blk, c)).wait_recv()
    for i, c in enumerate(every):
        remote(send_l, right_g.at[c], l_send.at[i], l_recv.at[c], (before, c)).wait_recv()
        remote(send_r, left_g.at[c], r_send.at[i], r_recv.at[c], (after, c)).wait_recv()
    own = own_g[0]
    left = left_g[0]
    right = right_g[0]
    for c in range(1, ncol):
        own = own + own_g[c]
        left = left + left_g[c]
        right = right + right_g[c]
    line = jnp.concatenate([own[:LAYERS], own[LAYERS:]], 1)
    line = jnp.concatenate([
        line[:, :LANES] + left[:LAYERS],
        line[:, LANES:HALF] + left[LAYERS:],
        line[:, HALF:pairs - HALF],
        line[:, pairs - HALF:pairs - LANES] + right[:LAYERS],
        line[:, pairs - LANES:] + right[LAYERS:],
    ], 1)
    grad[...] = line


def on_device(nblk, ncol, slab, angles, pairing, band_offsets, band_weights):
    rows, width = slab.shape
    halves = width // LANES
    pairs = rows // 2
    total_q = pairs + REACH
    buf_q = total_q + 8
    f32 = jnp.float32
    dma = pltpu.SemaphoreType.DMA
    smem = pl.BlockSpec(memory_space=pltpu.SMEM)
    anywhere = pl.BlockSpec(memory_space=pl.ANY)
    return pl.pallas_call(
        functools.partial(kernel, nblk, ncol),
        out_shape=(
            pltpu.VMEM((rows, width), f32),
            pltpu.VMEM((LAYERS, pairs), f32),
        ),
        in_specs=[smem, smem, smem, anywhere, anywhere],
        out_specs=(pl.BlockSpec(memory_space=pltpu.VMEM), pl.BlockSpec(memory_space=pltpu.VMEM)),
        scratch_shapes=[
            pltpu.VMEM((halves, FRONT + rows + SENT + 16, LANES), f32),
            pltpu.VMEM((halves, 2, 8, LANES), f32),
            pltpu.VMEM((halves, 2, HALF, LANES), f32),
            pltpu.VMEM((LAYERS, total_q), f32),
            pltpu.VMEM((2 * LAYERS, total_q, LANES), f32),
            pltpu.VMEM((halves, LAYERS - 1, buf_q, LANES), f32),
            pltpu.VMEM((halves, LAYERS - 1, buf_q, LANES), f32),
            pltpu.VMEM((halves, rows + 2 * REACH + 16, LANES), f32),
            pltpu.VMEM((2 * REACH + 8, LANES), f32),
            pltpu.VMEM((REACH + HALF + 24, LANES), f32),
            pltpu.VMEM((REACH + HALF, LANES), f32),
            pltpu.VMEM((halves, rows + 2 * REACH + 16, LANES), f32),
            pltpu.VMEM((halves, LAYERS - 1, buf_q, LANES), f32),
            pltpu.VMEM((halves, LAYERS - 1, buf_q, LANES), f32),
            pltpu.VMEM((halves, LAYERS, total_q, LANES), f32),
            pltpu.VMEM((2 * LAYERS, total_q), f32),
            pltpu.VMEM((ncol, 2 * LAYERS, pairs // 2), f32),
            pltpu.VMEM((ncol, 2 * LAYERS, LANES), f32),
            pltpu.VMEM((ncol, 2 * LAYERS, LANES), f32),
            pltpu.VMEM((2 * LAYERS, LANES), f32),
            pltpu.VMEM((2 * LAYERS, LANES), f32),
            dma((halves,)), dma,
            dma((halves, 2)), dma((halves, 2)),
            dma((halves, 2)), dma((halves, 2)),
            dma((2,)), dma((2,)),
            dma((ncol - 1,)), dma((ncol,)),
            dma((ncol,)), dma((ncol,)),
            dma((ncol,)), dma((ncol,)),
        ],
        compiler_params=pltpu.CompilerParams(
            collective_id=0, has_side_effects=True, vmem_limit_bytes=58 * 2**20),
    )(pairing, band_offsets, band_weights, slab, angles)


def solution(mesh):
    in_specs = (P("blk", "col"), P(None, "blk"), P(), P(), P())
    out_specs = (P("blk", "col"), P(None, "blk"))
    return jax.shard_map(
        functools.partial(on_device, mesh.shape["blk"], mesh.shape["col"]),
        mesh=mesh, in_specs=in_specs, out_specs=out_specs, check_vma=False,
    )
```

```python
import functools

import jax
import jax.numpy as jnp
from jax import lax
from jax.experimental import pallas as pl
from jax.experimental.pallas import tpu as pltpu
from jax.sharding import PartitionSpec as P

LAYERS = 4
BANDS = 8
REACH = 512
HALF = REACH // 2
SENT = HALF + 8
LANES = 128
FRONT = SENT + 8
MESH = pl.DeviceIdType.MESH


def sweep(low, high, step, body):
    assert (high - low) % step == 0 and low % 8 == 0 and step % 8 == 0
    if high - low == step:
        body(low)
        return

    def one(i, carry):
        body(pl.multiple_of(low + i * step, 8))
        return carry

    lax.fori_loop(0, (high - low) // step, one, 0)


def sin_cos(x):
    n = jnp.floor(x * 0.6366197723675814 + 0.5)
    r = ((x - n * 1.5703125) - n * 4.837512969970703e-4) - n * 7.54978995489188e-8
    z = r * r
    s = ((-1.9515295891e-4 * z + 8.3321608736e-3) * z - 1.6666654611e-1) * z * r + r
    c = ((2.443315711809948e-5 * z - 1.388731625493765e-3) * z + 4.166664568298827e-2) * z * z - 0.5 * z + 1.0
    odd = jnp.abs(n) == 1.0
    even_sign = jnp.where(n == 0.0, 1.0, -1.0)
    return jnp.where(odd, n * c, even_sign * s), jnp.where(odd, -n * s, even_sign * c)


def kernel(
    nblk, ncol,
    pairing, offsets, weights, slab, angles,
    out, grad,
    raw, near, far, angw, coef, sa, sb, field, left_f, right_f, cut, adj, xa, xb, prod, window,
    own_g, left_g, right_g, send_l, send_r,
    load_sem, ang_sem, n_send, n_recv, h_send, h_recv, a_send, a_recv,
    o_send, o_recv, l_send, l_recv, r_send, r_recv,
):
    rows, width = slab.shape
    halves = width // LANES
    pairs = rows // 2
    q_own = HALF
    q_end = q_own + pairs
    q_lo, q_hi = 120, q_end + 136
    total_q = pairs + REACH
    blk = lax.axis_index("blk")
    col = lax.axis_index("col")
    after = lax.rem(blk + 1, nblk)
    before = lax.rem(blk + nblk - 1, nblk)
    others = [lax.rem(col + d, ncol) for d in range(1, ncol)]
    every = [col] + others

    barrier = pltpu.get_barrier_semaphore()
    peers = [(b, c) for c in every for b in (after, before)] + [(blk, c) for c in others]
    for peer in peers:
        pl.semaphore_signal(barrier, inc=1, device_id=peer, device_id_type=MESH)

    loads = []
    for h in range(halves):
        loads.append(pltpu.make_async_copy(
            slab.at[:, pl.ds(h * LANES, LANES)], raw.at[h, pl.ds(FRONT, rows)], load_sem.at[h]))
    own_ang = pltpu.make_async_copy(angles, angw.at[:, pl.ds(HALF, pairs)], ang_sem)
    own_ang.start()
    for load in loads:
        load.start()

    def remote(src, dst, s, r, peer):
        return pltpu.make_async_remote_copy(
            src_ref=src, dst_ref=dst, send_sem=s, recv_sem=r, device_id=peer, device_id_type=MESH)

    ang_copies = [
        remote(angles.at[:, pl.ds(pairs - HALF, HALF)], angw.at[:, pl.ds(0, HALF)], a_send.at[0], a_recv.at[0], (after, col)),
        remote(angles.at[:, pl.ds(0, HALF)], angw.at[:, pl.ds(q_end, HALF)], a_send.at[1], a_recv.at[1], (before, col)),
    ]
    near_copies = []
    far_copies = []
    for h in range(halves):
        lanes = pl.ds(h * LANES, LANES)
        near_copies += [
            remote(slab.at[pl.ds(rows - 8, 8), lanes], near.at[h, 0], n_send.at[h, 0], n_recv.at[h, 0], (after, col)),
            remote(slab.at[pl.ds(0, 8), lanes], near.at[h, 1], n_send.at[h, 1], n_recv.at[h, 1], (before, col)),
        ]
        far_copies.append([
            remote(slab.at[pl.ds(rows - SENT, HALF), lanes], far.at[h, 0], h_send.at[h, 0], h_recv.at[h, 0], (after, col)),
            remote(slab.at[pl.ds(8, HALF), lanes], far.at[h, 1], h_send.at[h, 1], h_recv.at[h, 1], (before, col)),
        ])

    first = pairing[0]

    pl.semaphore_wait(barrier, len(peers))
    for copy in ang_copies + near_copies + far_copies[0]:
        copy.start()

    def zeros(n):
        return jnp.zeros((n, LANES), jnp.float32)

    left_f[...] = zeros(left_f.shape[0])
    right_f[...] = zeros(right_f.shape[0])
    cut[...] = zeros(cut.shape[0])
    for h in range(halves):
        raw[h, 0:8, :] = zeros(8)
        raw[h, FRONT + rows + SENT:FRONT + rows + SENT + 16, :] = zeros(16)
        adj[h, 2 * q_lo:REACH - HALF, :] = zeros(REACH - HALF - 2 * q_lo)
        top = REACH + rows + HALF
        adj[h, top:2 * q_hi + 8, :] = zeros(2 * q_hi + 8 - top)
        field[h, 0:REACH, :] = zeros(REACH)
        field[h, REACH + rows:, :] = zeros(field.shape[1] - REACH - rows)
        for l in range(LAYERS - 1):
            sa[h, l, q_hi:q_hi + 8, :] = zeros(8)
            sb[h, l, q_lo - 8:q_lo, :] = zeros(8)
            xb[h, l, q_lo - 8:q_lo, :] = zeros(8)
            xa[h, l, q_hi:q_hi + 8, :] = zeros(8)

    def coefficients(theta):
        mid = theta.shape[1] // 2
        sine, cosine = sin_cos(jnp.concatenate([theta[:, :mid], theta[:, mid:]], 0))
        return jnp.concatenate([
            jnp.concatenate([cosine[:LAYERS], sine[:LAYERS]], 0),
            jnp.concatenate([cosine[LAYERS:], sine[LAYERS:]], 0)], 1)

    def aligned(both):
        rolled = pltpu.roll(both, both.shape[1] - 1, 1)
        odd = lax.broadcasted_iota(jnp.int32, both.shape, 0) % 2 == 1
        moved = jnp.full(both.shape, first, jnp.int32) == 1
        return jnp.where(jnp.logical_and(odd, moved), rolled, both)

    def spread(q, low=0, n=LANES):
        turned = window[:, q:q + LANES].T[low:low + n]
        for j in range(2 * LAYERS):
            coef[j, q + low:q + low + n, :] = jnp.broadcast_to(turned[:, j:j + 1], (n, LANES))

    own_ang.wait()
    own_both = coefficients(angw[:, q_own:q_end])
    window[:, q_own:q_end] = aligned(own_both)
    for q in range(q_own, q_end - LANES, LANES):
        spread(q)

    def held(h, l, q, n):
        if l == LAYERS - 1:
            return adj[h, pl.ds(2 * q + 1, n, stride=2), :], adj[h, pl.ds(2 * q + 2, n, stride=2), :]
        if l % 2 == 1:
            return xb[h, l, pl.ds(q, n), :], xa[h, l, pl.ds(q + 1, n), :]
        return xb[h, l, pl.ds(q - 1, n), :], xa[h, l, pl.ds(q, n), :]

    def forward(halves_in, low, high, step, target, shift, products):
        for l in range(LAYERS):
            def body(q, l=l):
                c = coef[l, pl.ds(q, step), :]
                s = coef[LAYERS + l, pl.ds(q, step), :]
                for h in halves_in:
                    if l == 0:
                        a = raw[h, pl.ds(2 * q - 2 * q_lo + first, step, stride=2), :]
                        b = raw[h, pl.ds(2 * q - 2 * q_lo + 1 + first, step, stride=2), :]
                    elif l % 2 == 1:
                        a = sb[h, l - 1, pl.ds(q, step), :]
                        b = sa[h, l - 1, pl.ds(q + 1, step), :]
                    else:
                        a = sb[h, l - 1, pl.ds(q - 1, step), :]
                        b = sa[h, l - 1, pl.ds(q, step), :]
                    new_a = c * a - s * b
                    new_b = s * a + c * b
                    if l < LAYERS - 1:
                        sa[h, l, pl.ds(q, step), :] = new_a
                        sb[h, l, pl.ds(q, step), :] = new_b
                    if products:
                        a, b = held(h, l, q, step)
                        prod[h, l, pl.ds(q, step), :] = b * new_a - a * new_b
                    if l == LAYERS - 1:
                        into = target(h)
                        into[pl.ds(2 * q + 1 - shift, step, stride=2), :] = new_a
                        into[pl.ds(2 * q + 2 - shift, step, stride=2), :] = new_b
            sweep(low, high, step, body)

    reach = [offsets[k] for k in range(BANDS)]
    weight = [weights[k] for k in range(BANDS)]

    def band(h, low, high, upper=None, lower=None, shift=0, more=False):
        n = 128

        def body(t):
            acc = adj[h, pl.ds(t, n), :] if more else None
            for k in range(BANDS):
                part = None
                if upper is not None:
                    part = upper[pl.ds(t - shift + reach[k], n), :]
                if lower is not None:
                    down = lower[pl.ds(t - shift - reach[k], n), :]
                    part = down if part is None else part + down
                part = weight[k] * part
                acc = part if acc is None else acc + part
            adj[h, pl.ds(t, n), :] = acc
        sweep(low + REACH, high + REACH, n, body)

    def backward(halves_in, low, high, step, products):
        for l in reversed(range(LAYERS)):
            if l == 0 and not products:
                continue

            def body(q, l=l):
                if l > 0:
                    c = coef[l, pl.ds(q, step), :]
                    s = coef[LAYERS + l, pl.ds(q, step), :]
                for h in halves_in:
                    a, b = held(h, l, q, step)
                    if l > 0:
                        new_a = c * a + s * b
                        new_b = c * b - s * a
                        xa[h, l - 1, pl.ds(q, step), :] = new_a
                        xb[h, l - 1, pl.ds(q, step), :] = new_b
                    if products and l % 2 == 0:
                        prod[h, l, pl.ds(q, step), :] = b * sa[h, l, pl.ds(q, step), :] - a * sb[h, l, pl.ds(q, step), :]
                    elif products:
                        prod[h, l, pl.ds(q, step), :] = (
                            new_b * sb[h, l - 1, pl.ds(q, step), :] - new_a * sa[h, l - 1, pl.ds(q + 1, step), :])
            sweep(low, high, step, body)

    def collapse(q, n, more):
        start = q // LANES * LANES
        wanted = (lax.broadcasted_iota(jnp.int32, (n, LANES), 0) + (q - start)
                  == lax.broadcasted_iota(jnp.int32, (n, LANES), 1))
        for l in range(LAYERS):
            x = prod[0, l, q:q + n, :]
            for h in range(1, halves):
                x = x + prod[h, l, q:q + n, :]
            s = jnp.sum(x, axis=1, keepdims=True)
            line = jnp.sum(jnp.where(wanted, s, 0.0), axis=0, keepdims=True)
            if more:
                line = line + window[l:l + 1, start:start + LANES]
            window[l:l + 1, start:start + LANES] = line

    for load in loads:
        load.wait()
    for h in range(halves):
        forward([h], q_own, q_end - LANES, 112, lambda h: field.at[h], 0, False)
        if h == 0:
            for pair in far_copies[1:]:
                for copy in pair:
                    copy.start()

    for copy in ang_copies:
        copy.wait()
    left_both = coefficients(angw[:, :q_own])
    right_both = coefficients(angw[:, q_end:])
    window[...] = aligned(jnp.concatenate([left_both, own_both, right_both], 1))
    spread(0, q_lo, 8)
    for q in (LANES, q_end - LANES, q_end):
        spread(q)
    spread(q_end + LANES, 0, 8)
    for copy in near_copies:
        copy.wait()
    for h in range(halves):
        raw[h, FRONT - 8:FRONT, :] = near[h, 0]
        raw[h, FRONT + rows:FRONT + rows + 8, :] = near[h, 1]
    edge = REACH + rows
    for h in range(halves):
        forward([h], q_own - 8, q_own + 8, 16, lambda h: field.at[h], 0, False)
        forward([h], q_end - 136, q_end + 8, 144, lambda h: field.at[h], 0, False)

        def emit(r, h=h):
            out[pl.ds(r, 128), h * LANES:(h + 1) * LANES] = field[h, pl.ds(r + REACH - first, 128), :]

        sweep(0, rows, 128, emit)
        field[h, REACH - 16:REACH, :] = zeros(16)
        field[h, edge:edge + 24, :] = zeros(24)
        cut[0:HALF, :] = field[h, rows:rows + HALF, :]
        whole = field.at[h]
        band(h, -HALF, 0, upper=whole)
        band(h, 0, rows, upper=whole, lower=whole)
        band(h, rows, rows + HALF, lower=cut, shift=rows)
        backward([h], q_lo, q_own + 8, 144, False)
        backward([h], q_own + 248, q_end - 248, 176, True)
        backward([h], q_end - 136, q_hi, 136, True)
    collapse(q_own + 264, 120, False)
    for q in range(q_own + 384, q_end - 384, LANES):
        collapse(q, LANES, False)
    collapse(q_end - 384, 120, False)
    collapse(q_end - 120, 120, False)

    for h in range(halves):
        for copy in far_copies[h]:
            copy.wait()
        raw[h, 8:8 + HALF, :] = far[h, 0]
        raw[h, FRONT + rows + 8:FRONT + rows + SENT, :] = far[h, 1]
        forward([h], q_lo, q_own, 136, lambda h: left_f, 0, True)
        forward([h], q_end - 8, q_hi, 144, lambda h: right_f, rows, True)
        left_f[2 * q_lo:HALF, :] = zeros(HALF - 2 * q_lo)
        left_f[REACH:REACH + 8, :] = zeros(8)
        right_f[REACH - 16:REACH, :] = zeros(16)
        right_f[REACH + HALF:REACH + HALF + 24, :] = zeros(24)
        band(h, 0, REACH, lower=left_f, more=True)
        band(h, rows - REACH, rows - HALF, upper=right_f, shift=rows, more=True)
        backward([h], q_own - 8, q_own + 264, 136, True)
        backward([h], q_end - 264, q_end - 120, 144, True)
    collapse(q_lo, 8, False)
    collapse(LANES, LANES, False)
    collapse(q_own, LANES, False)
    collapse(q_own + LANES, LANES, False)
    collapse(q_own + HALF, 8, True)
    collapse(q_end - 264, 8, True)
    collapse(q_end - HALF, LANES, False)
    collapse(q_end - LANES, 8, True)
    collapse(q_end, LANES, False)
    collapse(q_end + LANES, 8, False)

    whole = window[...]
    rolled = pltpu.roll(whole, 1, 1)
    odd = lax.broadcasted_iota(jnp.int32, whole.shape, 0) % 2 == 1
    moved = jnp.full(whole.shape, first, jnp.int32) == 1
    whole = jnp.where(jnp.logical_and(odd, moved), rolled, whole)[:LAYERS]
    mid = q_own + pairs // 2
    own_g[pl.ds(col, 1)] = jnp.concatenate([whole[:, q_own:mid], whole[:, mid:q_end]], 0)[None]
    send_l[...] = jnp.concatenate([whole[:, 0:LANES], whole[:, LANES:HALF]], 0)
    send_r[...] = jnp.concatenate([whole[:, q_end:q_end + LANES], whole[:, q_end + LANES:]], 0)
    copies = []
    for i, c in enumerate(others):
        copies.append(remote(own_g.at[col], own_g.at[col], o_send.at[i], o_recv.at[col], (blk, c)))
    for i, c in enumerate(every):
        copies.append(remote(send_l, right_g.at[col], l_send.at[i], l_recv.at[col], (before, c)))
        copies.append(remote(send_r, left_g.at[col], r_send.at[i], r_recv.at[col], (after, c)))
    for copy in copies:
        copy.start()
    for copy in copies:
        copy.wait_send()
    for i, c in enumerate(others):
        remote(own_g.at[c], own_g.at[c], o_send.at[i], o_recv.at[c], (blk, c)).wait_recv()
    for i, c in enumerate(every):
        remote(send_l, right_g.at[c], l_send.at[i], l_recv.at[c], (before, c)).wait_recv()
        remote(send_r, left_g.at[c], r_send.at[i], r_recv.at[c], (after, c)).wait_recv()
    own = own_g[0]
    left = left_g[0]
    right = right_g[0]
    for c in range(1, ncol):
        own = own + own_g[c]
        left = left + left_g[c]
        right = right + right_g[c]
    line = jnp.concatenate([own[:LAYERS], own[LAYERS:]], 1)
    line = jnp.concatenate([
        line[:, :LANES] + left[:LAYERS],
        line[:, LANES:HALF] + left[LAYERS:],
        line[:, HALF:pairs - HALF],
        line[:, pairs - HALF:pairs - LANES] + right[:LAYERS],
        line[:, pairs - LANES:] + right[LAYERS:],
    ], 1)
    grad[...] = line


def on_device(nblk, ncol, slab, angles, pairing, band_offsets, band_weights):
    rows, width = slab.shape
    halves = width // LANES
    pairs = rows // 2
    total_q = pairs + REACH
    buf_q = total_q + 8
    f32 = jnp.float32
    dma = pltpu.SemaphoreType.DMA
    smem = pl.BlockSpec(memory_space=pltpu.SMEM)
    anywhere = pl.BlockSpec(memory_space=pl.ANY)
    return pl.pallas_call(
        functools.partial(kernel, nblk, ncol),
        out_shape=(
            pltpu.VMEM((rows, width), f32),
            pltpu.VMEM((LAYERS, pairs), f32),
        ),
        in_specs=[smem, smem, smem, anywhere, anywhere],
        out_specs=(pl.BlockSpec(memory_space=pltpu.VMEM), pl.BlockSpec(memory_space=pltpu.VMEM)),
        scratch_shapes=[
            pltpu.VMEM((halves, FRONT + rows + SENT + 16, LANES), f32),
            pltpu.VMEM((halves, 2, 8, LANES), f32),
            pltpu.VMEM((halves, 2, HALF, LANES), f32),
            pltpu.VMEM((LAYERS, total_q), f32),
            pltpu.VMEM((2 * LAYERS, total_q, LANES), f32),
            pltpu.VMEM((halves, LAYERS - 1, buf_q, LANES), f32),
            pltpu.VMEM((halves, LAYERS - 1, buf_q, LANES), f32),
            pltpu.VMEM((halves, rows + 2 * REACH + 16, LANES), f32),
            pltpu.VMEM((2 * REACH + 8, LANES), f32),
            pltpu.VMEM((REACH + HALF + 24, LANES), f32),
            pltpu.VMEM((REACH + HALF, LANES), f32),
            pltpu.VMEM((halves, rows + 2 * REACH + 16, LANES), f32),
            pltpu.VMEM((halves, LAYERS - 1, buf_q, LANES), f32),
            pltpu.VMEM((halves, LAYERS - 1, buf_q, LANES), f32),
            pltpu.VMEM((halves, LAYERS, total_q, LANES), f32),
            pltpu.VMEM((2 * LAYERS, total_q), f32),
            pltpu.VMEM((ncol, 2 * LAYERS, pairs // 2), f32),
            pltpu.VMEM((ncol, 2 * LAYERS, LANES), f32),
            pltpu.VMEM((ncol, 2 * LAYERS, LANES), f32),
            pltpu.VMEM((2 * LAYERS, LANES), f32),
            pltpu.VMEM((2 * LAYERS, LANES), f32),
            dma((halves,)), dma,
            dma((halves, 2)), dma((halves, 2)),
            dma((halves, 2)), dma((halves, 2)),
            dma((2,)), dma((2,)),
            dma((ncol - 1,)), dma((ncol,)),
            dma((ncol,)), dma((ncol,)),
            dma((ncol,)), dma((ncol,)),
        ],
        compiler_params=pltpu.CompilerParams(
            collective_id=0, has_side_effects=True, vmem_limit_bytes=58 * 2**20),
    )(pairing, band_offsets, band_weights, slab, angles)


def solution(mesh):
    in_specs = (P("blk", "col"), P(None, "blk"), P(), P(), P())
    out_specs = (P("blk", "col"), P(None, "blk"))
    return jax.shard_map(
        functools.partial(on_device, mesh.shape["blk"], mesh.shape["col"]),
        mesh=mesh, in_specs=in_specs, out_specs=out_specs, check_vma=False,
    )
```
